256 devices in a mesh: dp: 32 (over y, z_lo, core), seq: 8 (over z_hi, x).
Axes of the slice: x: 4, y: 4, z: 8 (z_hi: 2, z_lo: 4; z = z_hi * 4 + z_lo), core: 2. Of those that a mesh axis runs over, the one named last changes fastest.
Arguments:
- x_img: bfloat16 [32, 1024, 3072], P('dp', 'seq'), may hold values from -6 to 6
- txt_qkv: bfloat16 [32, 128, 6144], P('dp', None, 'seq'), may hold values from -6 to 6
- w_qkv: bfloat16 [3072, 6144], P('dp', 'seq'), may hold values from -0.109375 to 0.109375
- q_gain: float32 [128], replicated, may hold values from 0.5 to 1.5
- k_gain: float32 [128], replicated, may hold values from 0.5 to 1.5
- d_out: bfloat16 [32, 1152, 2048], P('dp', None, 'seq'), may hold values from -6 to 6
Outputs:
- grad_w: float32 [3072, 6144], P('dp', 'seq')
- grad_txt: bfloat16 [32, 128, 6144], P('dp', None, 'seq')
The draws below stay inside these ranges and needn't reach their ends.
All inputs are finite; a program needn't handle non-finite values.
Results may differ from the reference program's by a relative error of at most 0.03.
Values may be sent and summed in bfloat16 or wider, within the bound.
A program may use at most 64 MiB of HBM per device.

```python
import jax
import jax.numpy as jnp
from jax import lax

D = 3072
H = 16
HD = 128
TXT = 128
IMAGES = 32
IMG_SEQ = 1024
SEQ = 1152
COLS = 6144


def levels(rng, shape, cuts, smallest, largest):
    def one(dim, shards_of):
        draws = jax.random.uniform(jax.random.fold_in(jax.random.fold_in(rng, 6), dim), (shards_of,), jnp.float32, smallest / len(cuts), largest / len(cuts))
        return jnp.repeat(jnp.exp(draws), shape[dim] // shards_of).reshape((-1,) + (1,) * (len(shape) - dim - 1))

    loudness = one(*cuts[0])
    for cut in cuts[1:]:
        loudness = loudness * one(*cut)
    return loudness


def gaussian(key, extent, deviation, reach, shards=(), kind=jnp.bfloat16):
    values = jax.random.normal(key, extent, jnp.float32) * deviation
    if len(shards) > 0:
        values = levels(key, extent, shards, -0.22, 0.18) * values
    return jnp.clip(values, min=-reach, max=reach).astype(kind)


def setup_inputs(seed: int = 0) -> dict:
    seeds = jax.random.split(jax.random.key(seed), 7)
    x_img = gaussian(seeds[0], (IMAGES, IMG_SEQ, D), 1.0, 6.0, ((0, 32), (1, 8)))
    txt_qkv = gaussian(seeds[1], (IMAGES, TXT, COLS), 1.0, 6.0, ((0, 32), (2, 8)))
    w_qkv = gaussian(seeds[2], (D, COLS), D ** -0.5, 0.109375, ((0, 32), (1, 8)))
    q_gain = jnp.clip(1.0 + 0.1 * jax.random.normal(seeds[3], (HD,), jnp.float32), 0.5, 1.5)
    k_gain = jnp.clip(1.0 + 0.1 * jax.random.normal(seeds[4], (HD,), jnp.float32), 0.5, 1.5)
    d_out = gaussian(seeds[5], (IMAGES, SEQ, H * HD), 1.0, 6.0, ((0, 32), (2, 8)))
    return dict(x_img=x_img, txt_qkv=txt_qkv, w_qkv=w_qkv, q_gain=q_gain, k_gain=k_gain, d_out=d_out)


def head_grads(query_rows, key_rows, value_rows, grad_rows, q_gain, k_gain):
    scaling = query_rows.shape[-1] ** (-0.5)
    query_f = query_rows.astype(jnp.float32)
    key_f = key_rows.astype(jnp.float32)
    query_inv = lax.rsqrt(lax.optimization_barrier(jnp.mean(query_f * query_f, -1, keepdims=True)) + 1e-06)
    key_inv = lax.rsqrt(lax.optimization_barrier(jnp.mean(key_f * key_f, -1, keepdims=True)) + 1e-06)
    query_unit = query_f * query_inv
    key_unit = key_f * key_inv
    query_norm = (query_unit * q_gain).astype(jnp.bfloat16)
    key_norm = (key_unit * k_gain).astype(jnp.bfloat16)
    scores = jnp.dot(query_norm, key_norm.T, preferred_element_type=jnp.float32) * scaling
    powers = jnp.exp(scores)
    softmax = powers / lax.optimization_barrier(jnp.sum(powers, -1, keepdims=True))
    softmax_low = softmax.astype(jnp.bfloat16)
    value_grad = jnp.dot(softmax_low.T, grad_rows, preferred_element_type=jnp.float32)
    prob_grad = jnp.dot(grad_rows, value_rows.T, preferred_element_type=jnp.float32)
    centre = lax.optimization_barrier(jnp.sum(softmax * prob_grad, -1, keepdims=True))
    score_grad = (softmax * (prob_grad - centre) * scaling).astype(jnp.bfloat16)
    qnorm_grad = jnp.dot(score_grad, key_norm, preferred_element_type=jnp.float32) * q_gain
    knorm_grad = jnp.dot(score_grad.T, query_norm, preferred_element_type=jnp.float32) * k_gain
    query_grad = query_inv * (qnorm_grad - query_unit * lax.optimization_barrier(jnp.mean(qnorm_grad * query_unit, -1, keepdims=True)))
    key_grad = key_inv * (knorm_grad - key_unit * lax.optimization_barrier(jnp.mean(knorm_grad * key_unit, -1, keepdims=True)))
    return jnp.stack([query_grad, key_grad, value_grad], 1).astype(jnp.bfloat16)

def attention_grads(joined, grad_out, q_gain, k_gain, head_count):
    length_all = joined.shape[0]
    stacked = joined.reshape(length_all, head_count, 3, -1).transpose(1, 0, 2, 3)
    grad_heads = grad_out.reshape(length_all, head_count, -1).transpose(1, 0, 2)

    def single_head(items):
        return head_grads(items[0][:, 0], items[0][:, 1], items[0][:, 2], items[1], q_gain, k_gain)
    result = lax.map(single_head, (stacked, grad_heads))
    return result.transpose(1, 0, 2, 3).reshape(length_all, -1)

def reference(x_img, txt_qkv, w_qkv, q_gain, k_gain, d_out):

    def per_image(running, inputs):
        image_rows, text_rows, grad_rows = inputs
        projected = jnp.dot(image_rows, w_qkv, preferred_element_type=jnp.float32).astype(jnp.bfloat16)
        joined = jnp.concatenate([text_rows, projected], 0)
        qkv_grad = attention_grads(joined, grad_rows, q_gain, k_gain, H)
        running = running + lax.dot_general(image_rows, qkv_grad[TXT:], (((0,), (0,)), ((), ())), preferred_element_type=jnp.float32)
        return (running, qkv_grad[:TXT])
    zero_sum = jnp.zeros((D, 3 * H * HD), jnp.float32)
    grad_w, grad_txt = lax.scan(per_image, zero_sum, (x_img, txt_qkv, d_out))
    return (grad_w, grad_txt)
```

```python
import jax
import jax.numpy as jnp
from jax import lax
from jax.experimental import pallas as pl
from jax.experimental.pallas import tpu as pltpu
from jax.sharding import PartitionSpec as P

F32, BF16 = jnp.float32, jnp.bfloat16
MESH = pl.DeviceIdType.MESH
D, HD, TXT, SEQ, IMG = 3072, 128, 128, 1152, 1024
HC = 3 * HD
SCALE = HD ** -0.5
LOG2E = 1.4426950408889634
NT = (((1,), (1,)), ((), ()))
TN = (((0,), (0,)), ((), ()))


def dot(a, b, dims=(((1,), (0,)), ((), ()))):
    return lax.dot_general(a, b, dims, preferred_element_type=F32)


def ds(start, size, align):
    return pl.ds(pl.multiple_of(start, align), size)


def project(x, w, joined, first, count, tile):
    def body(t, _):
        r = first + t * tile
        joined[ds(TXT + r, tile, 128), :] = dot(x[ds(r, tile, 128), :], w[...]).astype(BF16)
        return 0

    lax.fori_loop(0, count // tile, body, 0)


def unit_rows(rows):
    rows = rows.astype(F32)
    inverse = lax.rsqrt(jnp.mean(rows * rows, -1, keepdims=True) + 1e-6)
    return rows * inverse, inverse


def attention_start(joined, qg, kg, qn, kn, knt, dk, dv):
    qn[...] = (unit_rows(joined[:, 0:HD])[0] * qg).astype(BF16)
    keys = (unit_rows(joined[:, HD:2 * HD])[0] * kg).astype(BF16)
    kn[...] = keys
    knt[...] = keys.T
    dk[...] = jnp.zeros_like(dk)
    dv[...] = jnp.zeros_like(dv)


def attention_block(joined, dout, qn, kn, knt, dqt, dk, dv, first, count):
    cols = pl.ds(first, count)
    qb, gb = qn[cols, :], dout[cols, :]
    powers = jnp.exp2(dot(kn[...], qb, NT) * (SCALE * LOG2E))
    inverse = 1.0 / jnp.sum(powers, 0, keepdims=True)
    dp = dot(joined[:, 2 * HD:], gb, NT)
    centre = jnp.sum(powers * dp, 0, keepdims=True) * inverse
    probs = (powers * inverse).astype(BF16)
    dscore = (powers * (dp - centre) * (inverse * SCALE)).astype(BF16)
    dv[...] += dot(probs, gb)
    dk[...] += dot(dscore, qb)
    dqt[:, cols] = dot(knt[...], dscore)


def attention_end(joined, qg, kg, dqt, dk, dv, grads):
    for at, gain, grad in ((0, qg, dqt[...].T), (HD, kg, dk[...])):
        unit, inverse = unit_rows(joined[:, at:at + HD])
        grad = grad * gain
        grad = inverse * (grad - unit * jnp.mean(grad * unit, -1, keepdims=True))
        grads[:, at:at + HD] = grad.astype(BF16)
    grads[:, 2 * HD:] = dv[...].astype(BF16)


class Net:
    def __init__(self, send_sems, recv_sems):
        self.sems, self.count, self.open = (send_sems, recv_sems), 0, []

    def send(self, src, dst, device):
        i = self.count
        self.count += 1
        copy = pltpu.make_async_remote_copy(
            src_ref=src, dst_ref=dst, send_sem=self.sems[0].at[i], recv_sem=self.sems[1].at[i],
            device_id=device, device_id_type=MESH)
        copy.start()
        self.open.append(copy)
        return copy

    def finish(self):
        for copy in self.open:
            copy.wait_send()


NSEM = 96


def make_kernel(upto):
    def kernel(x_ref, t_ref, w_ref, qg_ref, kg_ref, d_ref, gw_ref, gt_ref,
               xs, wg, joined, grads, dout, qn, kn, knt, dqt, dk, dv, acc, gb,
               from_a, from_b, from_l, from_r, zs, zr, tot, sib_w, sib_t, lsem, ssem, rsem):
        dp, seq = lax.axis_index("dp"), lax.axis_index("seq")
        c, zl, y = dp % 2, (dp // 2) % 4, dp // 8
        x, zh = seq % 4, seq // 4
        s = 1 - c
        chip = y * 4 + zl

        def at(yy, zz, cc):
            return {"dp": ((yy % 4) * 4 + zz % 4) * 2 + cc, "seq": seq}

        sib = at(y, zl, s)
        x_right = {"dp": dp, "seq": zh * 4 + (x + 1) % 4}
        x_left = {"dp": dp, "seq": zh * 4 + (x + 3) % 4}
        z_far = {"dp": dp, "seq": (1 - zh) * 4 + x}
        y_right, y_left = at(y + 1, zl, c), at(y + 3, zl, c)
        z_near = [at(y, zl + k, c) for k in (1, 2, 3)]
        qg, kg = qg_ref[...], kg_ref[...]

        local = [
            pltpu.make_async_copy(x_ref, xs.at[c, ds(seq * 128, 128, 128)], lsem.at[0]),
            pltpu.make_async_copy(w_ref.at[:, ds(c * HC, HC, 128)], wg.at[ds(chip * 192 + c * 96, 96, 32)], lsem.at[1]),
            pltpu.make_async_copy(d_ref.at[:, ds(c * HD, HD, 128)], dout.at[c], lsem.at[2]),
            pltpu.make_async_copy(t_ref.at[:, ds(c * HC, HC, 128)], joined.at[c, pl.ds(0, TXT)], lsem.at[3]),
        ]
        for copy in local:
            copy.start()
        barrier = pltpu.get_barrier_semaphore()
        peers = [sib, x_right, x_left, z_far, y_right, y_left] + z_near
        for peer in peers:
            pl.semaphore_signal(barrier, inc=1, device_id=peer, device_id_type=MESH)
        pl.semaphore_wait(barrier, len(peers))
        net = Net(ssem, rsem)

        def xrows(image, slot, half, part=None):
            start = slot * 128 + half * 64
            if part is None:
                return xs.at[image, ds(start, 64, 64)]
            return xs.at[image, ds(start + part * 32, 32, 32)]

        class Ring:
            def __init__(self, image, group, source=None):
                self.image, self.base = image, group * 4
                self.mine = self.base + x
                self.left, self.right = self.base + (x + 3) % 4, self.base + (x + 1) % 4
                self.far = self.base + (x + 2) % 4
                self.source = source or (lambda part: xrows(image, self.mine, c, part))
                self.to_right, self.to_left = {}, {}

            def send(self, part, first_right):
                for right in (first_right, not first_right):
                    table, device = (self.to_right, x_right) if right else (self.to_left, x_left)
                    table[part] = net.send(self.source(part), xrows(self.image, self.mine, c, part), device)

            def forward(self):
                self.to_right[0].wait_recv()
                block = xrows(self.image, self.left, c, 0)
                self.on_right = net.send(block, block, x_right)
                self.to_left[1].wait_recv()
                block = xrows(self.image, self.right, c, 1)
                self.on_left = net.send(block, block, x_left)

            def share_near(self):
                self.to_right[1].wait_recv()
                self.to_left[0].wait_recv()
                self.shared = [share(self.image, slot) for slot in (self.left, self.right)]

            def share_far(self):
                self.on_right.wait_recv()
                self.on_left.wait_recv()
                self.shared.append(share(self.image, self.far))

            def arrived(self):
                for copy in self.shared:
                    copy.wait_recv()

        def share(image, slot):
            block = xrows(image, slot, c)
            return net.send(block, block, sib)

        w_sib = net.send(w_ref.at[:, ds(s * HC, HC, 128)], wg.at[ds(chip * 192 + c * 96, 96, 32)], sib)
        x_sib = [net.send(x_ref.at[ds(h * 64, 64, 64)], xrows(c, seq, h), sib) for h in (s, c)]
        ring_c = Ring(c, zh, lambda part: x_ref.at[ds(c * 64 + part * 32, 32, 32)])
        ring_c.send(0, True)
        ring_c.send(1, False)
        d_sib = net.send(d_ref.at[:, ds(s * HD, HD, 128)], dout.at[c], sib)
        t_sib = net.send(t_ref.at[:, ds(s * HC, HC, 128)], joined.at[c, pl.ds(0, TXT)], sib)

        local[1].wait()
        w_sib.wait_recv()
        block = wg.at[ds(chip * 192, 192, 64)]
        w_near = [net.send(block, block, peer) for peer in z_near]
        local[0].wait()
        x_sib[0].wait_recv()
        ring_s = Ring(s, zh)
        ring_s.send(0, True)
        ring_s.send(1, False)

        def z_send(image):
            return [net.send(xrows(image, seq, c, part), xrows(image, seq, c, part), z_far) for part in (0, 1)]

        def wrows(group, part):
            return wg.at[ds((group % 4) * 768 + part * 384, 384, 128)]

        if upto >= 1:
            for copy in w_near:
                copy.wait_recv()
            wr0 = net.send(wrows(y, 0), wrows(y, 0), y_right)
            wl1 = net.send(wrows(y, 1), wrows(y, 1), y_left)
            wr1 = net.send(wrows(y, 1), wrows(y, 1), y_right)
            wl0 = net.send(wrows(y, 0), wrows(y, 0), y_left)
            z0 = z_send(0)
        ring_c.forward()
        ring_s.forward()
        if upto >= 1:
            wr0.wait_recv()
            wrr = net.send(wrows(y + 3, 0), wrows(y + 3, 0), y_right)
            wl1.wait_recv()
            wll = net.send(wrows(y + 1, 1), wrows(y + 1, 1), y_left)
            ring0 = Ring(0, 1 - zh)
            ring1 = Ring(1, 1 - zh)
            z0[0].wait_recv()
            ring0.send(0, True)
            z1 = z_send(1)
            z0[1].wait_recv()
            ring0.send(1, False)
            far0 = share(0, ring0.mine)
        ring_c.share_near()
        ring_s.share_near()
        ring_c.share_far()
        ring_s.share_far()
        if upto >= 1:
            z1[0].wait_recv()
            ring1.send(0, True)
            ring0.forward()
            z1[1].wait_recv()
            ring1.send(1, False)
            far1 = share(1, ring1.mine)
            for copy in (wr1, wl0, wrr, wll):
                copy.wait_recv()
        x_sib[1].wait_recv()
        d_sib.wait_recv()
        t_sib.wait_recv()
        local[2].wait()
        local[3].wait()
        ring_c.arrived()
        ring_s.arrived()

        def attend(image, hooks):
            attention_start(joined.at[image], qg, kg, qn, kn, knt, dk, dv)
            for i, hook in enumerate(hooks):
                attention_block(joined.at[image], dout.at[image], qn, kn, knt, dqt, dk, dv,
                                i * (SEQ // len(hooks)), SEQ // len(hooks))
                if hook is not None:
                    hook()
            attention_end(joined.at[image], qg, kg, dqt, dk, dv, grads.at[image])

        if upto >= 1:
            if upto >= 2:
                project(xs.at[0], wg, joined.at[0], zh * 512, 512, 512)
            ring0.share_near()
            ring0.share_far()
            if upto >= 2:
                project(xs.at[1], wg, joined.at[1], zh * 512, 512, 512)
            far0.wait_recv()
            ring0.arrived()
            if upto >= 2:
                project(xs.at[0], wg, joined.at[0], (1 - zh) * 512, 512, 512)
            ring1.forward()
            if upto >= 3:
                attend(0, [None, ring1.share_near, None])
            else:
                ring1.share_near()
            ring1.share_far()
            if upto >= 4:
                def early(t, _):
                    cols = ds(t * 768, 768, 128)
                    acc[cols, :] = dot(xs[0, :, cols], grads[0, TXT:, :], TN)
                    return 0
                lax.fori_loop(0, 4, early, 0)
            far1.wait_recv()
            ring1.arrived()
            if upto >= 2:
                project(xs.at[1], wg, joined.at[1], (1 - zh) * 512, 512, 512)
            if upto >= 3:
                attend(1, [None, None, None])
                text = net.send(grads.at[s, pl.ds(0, TXT)], sib_t, sib)

        def late(group):
            cols = ds((group % 4) * 768, 768, 128)
            total = acc[cols, :] + dot(xs[1, :, cols], grads[1, TXT:, :], TN)
            acc[cols, :] = total
            gb[cols, :] = total.astype(BF16)

        def grows(group, part):
            return ds((group % 4) * 768 + part * 384, 384, 128)

        lo, hi = pl.ds(0, 384), pl.ds(384, 384)
        if upto >= 4:
            late(y + 2)
            if upto >= 5:
                ga = net.send(gb.at[grows(y + 2, 0)], from_a, y_right)
                gl = net.send(gb.at[grows(y + 2, 1)], from_b, y_left)
            late(y + 1)
            if upto >= 5:
                r1 = net.send(gb.at[grows(y + 1, 1)], from_l.at[hi], y_right)
            late(y + 3)
            if upto >= 5:
                l0 = net.send(gb.at[grows(y + 3, 0)], from_r.at[lo], y_left)
                ga.wait_recv()
                rows = grows(y + 1, 0)
                gb[rows, :] = (acc[rows, :] + from_a[...].astype(F32)).astype(BF16)
                r0 = net.send(gb.at[rows], from_l.at[lo], y_right)
                gl.wait_recv()
                rows = grows(y + 3, 1)
                gb[rows, :] = (acc[rows, :] + from_b[...].astype(F32)).astype(BF16)
                l1 = net.send(gb.at[rows], from_r.at[hi], y_left)
            late(y)
            if upto >= 5:
                for part, copies in ((0, (l0, r0)), (1, (r1, l1))):
                    for copy in copies:
                        copy.wait_recv()
                    rows, half = grows(y, part), pl.ds(part * 384, 384)
                    total = acc[rows, :] + from_l[half, :].astype(F32) + from_r[half, :].astype(F32)
                    acc[rows, :] = total
                    zs[half, :] = total.astype(BF16)
                gz = [net.send(zs.at[ds(((zl + k) % 4) * 192, 192, 64)], zr.at[k - 1], z_near[k - 1]) for k in (1, 2, 3)]
                for copy in gz:
                    copy.wait_recv()
                total = acc[ds(chip * 192, 192, 64), :]
                for k in range(3):
                    total = total + zr[k].astype(F32)
                tot[...] = total
                last = net.send(tot.at[ds(s * 96, 96, 32)], sib_w, sib)
                gw_ref[:, ds(c * HC, HC, 128)] = tot[ds(c * 96, 96, 32), :]
                last.wait_recv()
                gw_ref[:, ds(s * HC, HC, 128)] = sib_w[...]
        if upto >= 3:
            text.wait_recv()
            gt_ref[:, ds(c * HC, HC, 128)] = grads[c, 0:TXT, :]
            gt_ref[:, ds(s * HC, HC, 128)] = sib_t[...]
        net.finish()

    return kernel


def make_device(upto=9):
    def per_device(x_img, txt_qkv, w_qkv, q_gain, k_gain, d_out):
        hbm, vmem = pl.BlockSpec(memory_space=pl.ANY), pl.BlockSpec(memory_space=pltpu.VMEM)
        grad_w, grad_t = pl.pallas_call(
            make_kernel(upto),
            name="joint_block",
            out_shape=(jax.ShapeDtypeStruct((96, 2 * HC), F32), jax.ShapeDtypeStruct((TXT, 2 * HC), BF16)),
            in_specs=[hbm, hbm, hbm, vmem, vmem, hbm],
            out_specs=(vmem, vmem),
            scratch_shapes=[
                pltpu.VMEM((2, IMG, D), BF16),
                pltpu.VMEM((D, HC), BF16),
                pltpu.VMEM((2, SEQ, HC), BF16),
                pltpu.VMEM((2, SEQ, HC), BF16),
                pltpu.VMEM((2, SEQ, HD), BF16),
                pltpu.VMEM((SEQ, HD), BF16),
                pltpu.VMEM((SEQ, HD), BF16),
                pltpu.VMEM((HD, SEQ), BF16),
                pltpu.VMEM((HD, SEQ), F32),
                pltpu.VMEM((SEQ, HD), F32),
                pltpu.VMEM((SEQ, HD), F32),
                pltpu.VMEM((D, HC), F32),
                pltpu.VMEM((D, HC), BF16),
                pltpu.VMEM((384, HC), BF16),
                pltpu.VMEM((384, HC), BF16),
                pltpu.VMEM((768, HC), BF16),
                pltpu.VMEM((768, HC), BF16),
                pltpu.VMEM((768, HC), BF16),
                pltpu.VMEM((3, 192, HC), BF16),
                pltpu.VMEM((192, HC), F32),
                pltpu.VMEM((96, HC), F32),
                pltpu.VMEM((TXT, HC), BF16),
                pltpu.SemaphoreType.DMA((4,)),
                pltpu.SemaphoreType.DMA((NSEM,)),
                pltpu.SemaphoreType.DMA((NSEM,)),
            ],
            compiler_params=pltpu.CompilerParams(
                collective_id=0, has_side_effects=True, vmem_limit_bytes=60 * 2 ** 20),
        )(x_img[0], txt_qkv[0], w_qkv, q_gain.reshape(1, HD), k_gain.reshape(1, HD), d_out[0])
        return grad_w, grad_t[None]

    return per_device


def solution(mesh, upto=9):
    in_specs = (P("dp", "seq", None), P("dp", None, "seq"), P("dp", "seq"), P(), P(), P("dp", None, "seq"))
    out_specs = (P("dp", "seq"), P("dp", None, "seq"))
    return jax.shard_map(make_device(upto), mesh=mesh, in_specs=in_specs, out_specs=out_specs, check_vma=False)
```

```python
import jax
import jax.numpy as jnp
from jax import lax
from jax.experimental import pallas as pl
from jax.experimental.pallas import tpu as pltpu
from jax.sharding import PartitionSpec as P

F32, BF16 = jnp.float32, jnp.bfloat16
MESH = pl.DeviceIdType.MESH
D, HD, TXT, SEQ, IMG = 3072, 128, 128, 1152, 1024
HC = 3 * HD
SCALE = HD ** -0.5
LOG2E = 1.4426950408889634
NT = (((1,), (1,)), ((), ()))
TN = (((0,), (0,)), ((), ()))


def dot(a, b, dims=(((1,), (0,)), ((), ()))):
    return lax.dot_general(a, b, dims, preferred_element_type=F32)


def ds(start, size, align):
    return pl.ds(pl.multiple_of(start, align), size)


def project(x, w, joined, first, count, tile):
    def body(t, _):
        r = first + t * tile
        joined[ds(TXT + r, tile, 128), :] = dot(x[ds(r, tile, 128), :], w[...]).astype(BF16)
        return 0

    lax.fori_loop(0, count // tile, body, 0)


def unit_rows(rows):
    rows = rows.astype(F32)
    inverse = lax.rsqrt(jnp.mean(rows * rows, -1, keepdims=True) + 1e-6)
    return rows * inverse, inverse


def attention_start(joined, qg, kg, qn, kn, knt, dk, dv):
    qn[...] = (unit_rows(joined[:, 0:HD])[0] * qg).astype(BF16)
    keys = (unit_rows(joined[:, HD:2 * HD])[0] * kg).astype(BF16)
    kn[...] = keys
    knt[...] = keys.T
    dk[...] = jnp.zeros_like(dk)
    dv[...] = jnp.zeros_like(dv)


def attention_block(joined, dout, qn, kn, knt, dqt, dk, dv, first, count):
    cols = pl.ds(first, count)
    qb, gb = qn[cols, :], dout[cols, :]
    powers = jnp.exp2(dot(kn[...], qb, NT) * (SCALE * LOG2E))
    inverse = 1.0 / jnp.sum(powers, 0, keepdims=True)
    dp = dot(joined[:, 2 * HD:], gb, NT)
    centre = jnp.sum(powers * dp, 0, keepdims=True) * inverse
    probs = (powers * inverse).astype(BF16)
    dscore = (powers * (dp - centre) * (inverse * SCALE)).astype(BF16)
    dv[...] += dot(probs, gb)
    dk[...] += dot(dscore, qb)
    dqt[:, cols] = dot(knt[...], dscore)


def attention_end(joined, qg, kg, dqt, dk, dv, grads):
    for at, gain, grad in ((0, qg, dqt[...].T), (HD, kg, dk[...])):
        unit, inverse = unit_rows(joined[:, at:at + HD])
        grad = grad * gain
        grad = inverse * (grad - unit * jnp.mean(grad * unit, -1, keepdims=True))
        grads[:, at:at + HD] = grad.astype(BF16)
    grads[:, 2 * HD:] = dv[...].astype(BF16)


class Net:
    def __init__(self, send_sems, recv_sems):
        self.sems, self.count, self.open = (send_sems, recv_sems), 0, []

    def send(self, src, dst, device):
        i = self.count
        self.count += 1
        copy = pltpu.make_async_remote_copy(
            src_ref=src, dst_ref=dst, send_sem=self.sems[0].at[i], recv_sem=self.sems[1].at[i],
            device_id=device, device_id_type=MESH)
        copy.start()
        self.open.append(copy)
        return copy

    def finish(self):
        for copy in self.open:
            copy.wait_send()


PARTS = 4
PROWS = 64 // PARTS
NSEM = 122
BQ = 384


def make_kernel():
    def kernel(x_ref, t_ref, w_ref, qg_ref, kg_ref, d_ref, gw_ref, gt_ref,
               xs, wg, joined, grads, dout, qn, kn, knt, dqt, dk, dv, acc, gb,
               from_a, from_b, from_l, from_r, zs, zr, tot, sib_w, sib_t, lsem, done_sem, ssem, rsem):
        dp, seq = lax.axis_index("dp"), lax.axis_index("seq")
        c, zl, y = dp % 2, (dp // 2) % 4, dp // 8
        x, zh = seq % 4, seq // 4
        s = 1 - c
        chip = y * 4 + zl

        def at(yy, zz, cc):
            return {"dp": ((yy % 4) * 4 + zz % 4) * 2 + cc, "seq": seq}

        sib = at(y, zl, s)
        x_right = {"dp": dp, "seq": zh * 4 + (x + 1) % 4}
        x_left = {"dp": dp, "seq": zh * 4 + (x + 3) % 4}
        z_far = {"dp": dp, "seq": (1 - zh) * 4 + x}
        y_right, y_left = at(y + 1, zl, c), at(y + 3, zl, c)
        z_near = [at(y, zl + k, c) for k in (1, 2, 3)]
        qg, kg = qg_ref[...], kg_ref[...]

        local = [
            pltpu.make_async_copy(x_ref, xs.at[c, ds(seq * 128, 128, 128)], lsem.at[0]),
            pltpu.make_async_copy(w_ref.at[:, ds(c * HC, HC, 128)], wg.at[ds(chip * 192 + c * 96, 96, 32)], lsem.at[1]),
            pltpu.make_async_copy(d_ref.at[:, ds(c * HD, HD, 128)], dout.at[c], lsem.at[2]),
            pltpu.make_async_copy(t_ref.at[:, ds(c * HC, HC, 128)], joined.at[c, pl.ds(0, TXT)], lsem.at[3]),
        ]
        for copy in local:
            copy.start()
        barrier = pltpu.get_barrier_semaphore()
        peers = [sib, x_right, x_left, z_far, y_right, y_left] + z_near
        for peer in peers:
            pl.semaphore_signal(barrier, inc=1, device_id=peer, device_id_type=MESH)
        pl.semaphore_wait(barrier, len(peers))
        net = Net(ssem, rsem)

        def xrows(image, slot, half, part=None):
            start = slot * 128 + half * 64
            if part is None:
                return xs.at[image, ds(start, 64, 64)]
            return xs.at[image, ds(start + part * PROWS, PROWS, PROWS)]

        class Ring:
            def __init__(self, image, group, source=None):
                self.image = image
                slots = [group * 4 + (x + k) % 4 for k in range(4)]
                self.mine, self.right, self.far, self.left = slots
                self.source = source or (lambda part: xrows(image, self.mine, c, part))
                self.to_right, self.to_left, self.on = {}, {}, []

            def send(self, part):
                for right in (True, False) if part % 2 == 0 else (False, True):
                    table, device = (self.to_right, x_right) if right else (self.to_left, x_left)
                    table[part] = net.send(self.source(part), xrows(self.image, self.mine, c, part), device)

            def forward(self, part):
                table, slot, device = (
                    (self.to_right, self.left, x_right) if part % 2 == 0 else (self.to_left, self.right, x_left))
                table[part].wait_recv()
                block = xrows(self.image, slot, c, part)
                self.on.append(net.send(block, block, device))

            def share_near(self):
                for part in range(PARTS):
                    (self.to_left if part % 2 == 0 else self.to_right)[part].wait_recv()
                self.shared = [share(self.image, slot) for slot in (self.left, self.right)]

            def share_far(self):
                for copy in self.on:
                    copy.wait_recv()
                self.shared.append(share(self.image, self.far))

            def arrived(self):
                for copy in self.shared:
                    copy.wait_recv()

        def share(image, slot):
            block = xrows(image, slot, c)
            return net.send(block, block, sib)

        w_sib = net.send(w_ref.at[:, ds(s * HC, HC, 128)], wg.at[ds(chip * 192 + c * 96, 96, 32)], sib)
        x_sib = [net.send(x_ref.at[ds(h * 64, 64, 64)], xrows(c, seq, h), sib) for h in (s, c)]
        parts = range(PARTS)
        ring_c = Ring(c, zh, lambda part: x_ref.at[ds(c * 64 + part * PROWS, PROWS, PROWS)])
        for p in parts:
            ring_c.send(p)
        d_sib = net.send(d_ref.at[:, ds(s * HD, HD, 128)], dout.at[c], sib)
        t_sib = net.send(t_ref.at[:, ds(s * HC, HC, 128)], joined.at[c, pl.ds(0, TXT)], sib)

        y_ring = {}

        def y_send(k):
            block = wg.at[ds((y * 4 + (zl + 4 - k) % 4) * 192, 192, 64)]
            y_ring[k] = [net.send(block, block, y_right), net.send(block, block, y_left)]

        def y_forward(k):
            y_ring[k][k % 2].wait_recv()
            step, device = (3, y_right) if k % 2 == 0 else (1, y_left)
            block = wg.at[ds((((y + step) % 4) * 4 + (zl + 4 - k) % 4) * 192, 192, 64)]
            y_ring[k].append(net.send(block, block, device))

        def y_arrived(k):
            for copy in (y_ring[k][1 - k % 2], y_ring[k][2]):
                copy.wait_recv()

        local[1].wait()
        w_sib.wait_recv()
        block = wg.at[ds(chip * 192, 192, 64)]
        w_near = [net.send(block, block, peer) for peer in z_near]
        y_send(0)
        local[0].wait()
        x_sib[0].wait_recv()
        ring_s = Ring(s, zh)
        z = {}

        def z_send(u):
            if u >= 2:
                pl.semaphore_wait(done_sem.at[u - 2], 3)
            z[u] = net.send(*[xrows(u // PARTS, seq, c, u % PARTS)] * 2, z_far)

        def z_done(u):
            z[u].wait_recv()
            if u < 2 * PARTS - 2:
                for peer in z_near:
                    pl.semaphore_signal(done_sem.at[u], inc=1, device_id=peer, device_id_type=MESH)

        z_send(0)
        z_send(1)
        for p in parts:
            ring_s.send(p)
        for p in parts:
            ring_c.forward(p)
        y_forward(0)
        ring_s.forward(0)
        ring_s.forward(1)
        w_near[0].wait_recv()
        y_send(1)
        ring_s.forward(2)
        ring_s.forward(3)
        w_near[2].wait_recv()
        y_send(3)
        w_near[1].wait_recv()
        y_send(2)
        ring0, ring1 = Ring(0, 1 - zh), Ring(1, 1 - zh)

        def step(ring, part):
            z_done(ring.image * PARTS + part)
            ring.send(part)

        def slots(image, first, count):
            project(xs.at[image], wg, joined.at[image], first * 128, count * 128, count * 128)

        def start(image):
            attention_start(joined.at[image], qg, kg, qn, kn, knt, dk, dv)

        def block(image, i):
            attention_block(joined.at[image], dout.at[image], qn, kn, knt, dqt, dk, dv, i * BQ, BQ)

        def end(image):
            attention_end(joined.at[image], qg, kg, dqt, dk, dv, grads.at[image])

        def early(t):
            cols = pl.ds(t * 768, 768)
            acc[cols, :] = dot(xs[0, :, cols], grads[0, TXT:, :], TN)

        step(ring0, 0)
        step(ring0, 1)
        z_send(2)
        z_send(3)
        y_forward(1)
        ring_c.share_near()
        ring_s.share_near()
        ring0.forward(0)
        y_forward(3)
        y_forward(2)
        ring0.forward(1)
        step(ring0, 2)
        z_send(4)
        ring_c.share_far()
        ring_s.share_far()
        step(ring0, 3)
        z_send(5)
        ring0.forward(2)
        far0 = share(0, ring0.mine)
        x_sib[1].wait_recv()
        d_sib.wait_recv()
        t_sib.wait_recv()
        local[2].wait()
        local[3].wait()
        for k in range(4):
            y_arrived(k)
        ring_c.arrived()
        ring_s.arrived()
        slots(0, zh * 4, 4)
        ring0.forward(3)
        step(ring1, 0)
        z_send(6)
        slots(1, zh * 4, 4)
        ring0.share_near()
        step(ring1, 1)
        z_send(7)
        ring1.forward(0)
        ring0.share_far()
        far0.wait_recv()
        ring0.arrived()
        slots(0, (1 - zh) * 4, 4)
        start(0)
        step(ring1, 2)
        ring1.forward(1)
        block(0, 0)
        step(ring1, 3)
        far1 = share(1, ring1.mine)
        ring1.forward(2)
        block(0, 1)
        ring1.forward(3)
        ring1.share_near()
        block(0, 2)
        end(0)
        early(0)
        ring1.share_far()
        early(1)
        early(2)
        early(3)
        far1.wait_recv()
        slots(1, ring1.mine, 1)
        for copy, slot in zip(ring1.shared, (ring1.left, ring1.right, ring1.far)):
            copy.wait_recv()
            slots(1, slot, 1)
        start(1)
        for i in range(3):
            block(1, i)
        end(1)
        text = net.send(grads.at[s, pl.ds(0, TXT)], sib_t, sib)

        def late(group):
            cols = ds((group % 4) * 768, 768, 128)
            total = acc[cols, :] + dot(xs[1, :, cols], grads[1, TXT:, :], TN)
            acc[cols, :] = total
            gb[cols, :] = total.astype(BF16)

        right = [(1, 0), (1, 1), (3, 0), (0, 0)]
        left = [(2, 0), (2, 1), (3, 1), (0, 1)]

        def grows(group, piece):
            return ds((group % 4) * 768 + ((zl + piece[0]) % 4) * 192 + piece[1] * 96, 96, 32)

        class Way:
            def __init__(self, ahead, device, far, total, pieces, others):
                self.ahead, self.device, self.far, self.total = ahead, device, far, total
                self.pieces, self.others = pieces, others
                self.far_copy, self.added, self.near = {}, {}, {}

            def send_far(self, i):
                self.far_copy[i] = net.send(gb.at[grows(y + 2, self.pieces[i])], self.far.at[i], self.device)

            def send_near(self, i):
                self.near[i] = net.send(gb.at[grows(y + self.ahead, self.others[i])], self.total.at[4 + i], self.device)

            def send_added(self, i):
                self.far_copy[i].wait_recv()
                rows = grows(y + self.ahead, self.pieces[i])
                gb[rows, :] = (acc[rows, :] + self.far[i].astype(F32)).astype(BF16)
                self.added[i] = net.send(gb.at[rows], self.total.at[i], self.device)

        ways = (Way(1, y_right, from_a, from_l, right, left), Way(3, y_left, from_b, from_r, left, right))
        late(y + 2)
        for i in range(4):
            for way in ways:
                way.send_far(i)
        late(y + 1)
        late(y + 3)
        late(y)
        z_copies = []

        def complete(i):
            for way, other in (ways, ways[::-1]):
                way.added[i].wait_recv()
                other.near[i].wait_recv()
                piece = way.pieces[i]
                rows = grows(y, piece)
                total = acc[rows, :] + way.total[i].astype(F32) + other.total[4 + i].astype(F32)
                k, h = piece
                if k == 0:
                    acc[rows, :] = total
                else:
                    zs[k - 1, pl.ds(h * 96, 96), :] = total.astype(BF16)
                    z_copies.append(net.send(
                        zs.at[k - 1, pl.ds(h * 96, 96)], zr.at[k - 1, pl.ds(h * 96, 96)], z_near[k - 1]))

        for i in range(4):
            for way in ways:
                way.send_added(i)
                way.send_near(i)
            if i >= 1:
                complete(i - 1)
        complete(3)
        for copy in z_copies:
            copy.wait_recv()
        total = acc[ds(chip * 192, 192, 64), :]
        for k in range(3):
            total = total + zr[k].astype(F32)
        tot[...] = total
        last = net.send(tot.at[ds(s * 96, 96, 32)], sib_w, sib)
        gw_ref[:, ds(c * HC, HC, 128)] = tot[ds(c * 96, 96, 32), :]
        last.wait_recv()
        gw_ref[:, ds(s * HC, HC, 128)] = sib_w[...]
        text.wait_recv()
        gt_ref[:, ds(c * HC, HC, 128)] = grads[c, 0:TXT, :]
        gt_ref[:, ds(s * HC, HC, 128)] = sib_t[...]
        net.finish()

    return kernel


def make_device():
    def per_device(x_img, txt_qkv, w_qkv, q_gain, k_gain, d_out):
        hbm, vmem = pl.BlockSpec(memory_space=pl.ANY), pl.BlockSpec(memory_space=pltpu.VMEM)
        grad_w, grad_t = pl.pallas_call(
            make_kernel(),
            name="joint_block",
            out_shape=(jax.ShapeDtypeStruct((96, 2 * HC), F32), jax.ShapeDtypeStruct((TXT, 2 * HC), BF16)),
            in_specs=[hbm, hbm, hbm, vmem, vmem, hbm],
            out_specs=(vmem, vmem),
            scratch_shapes=[
                pltpu.VMEM((2, IMG, D), BF16),
                pltpu.VMEM((D, HC), BF16),
                pltpu.VMEM((2, SEQ, HC), BF16),
                pltpu.VMEM((2, SEQ, HC), BF16),
                pltpu.VMEM((2, SEQ, HD), BF16),
                pltpu.VMEM((SEQ, HD), BF16),
                pltpu.VMEM((SEQ, HD), BF16),
                pltpu.VMEM((HD, SEQ), BF16),
                pltpu.VMEM((HD, SEQ), F32),
                pltpu.VMEM((SEQ, HD), F32),
                pltpu.VMEM((SEQ, HD), F32),
                pltpu.VMEM((D, HC), F32),
                pltpu.VMEM((D, HC), BF16),
                pltpu.VMEM((4, 96, HC), BF16),
                pltpu.VMEM((4, 96, HC), BF16),
                pltpu.VMEM((8, 96, HC), BF16),
                pltpu.VMEM((8, 96, HC), BF16),
                pltpu.VMEM((3, 192, HC), BF16),
                pltpu.VMEM((3, 192, HC), BF16),
                pltpu.VMEM((192, HC), F32),
                pltpu.VMEM((96, HC), F32),
                pltpu.VMEM((TXT, HC), BF16),
                pltpu.SemaphoreType.DMA((4,)),
                pltpu.SemaphoreType.REGULAR((2 * PARTS - 2,)),
                pltpu.SemaphoreType.DMA((NSEM,)),
                pltpu.SemaphoreType.DMA((NSEM,)),
            ],
            compiler_params=pltpu.CompilerParams(
                collective_id=0, has_side_effects=True, vmem_limit_bytes=60 * 2 ** 20),
        )(x_img[0], txt_qkv[0], w_qkv, q_gain.reshape(1, HD), k_gain.reshape(1, HD), d_out[0])
        return grad_w, grad_t[None]

    return per_device


def solution(mesh):
    in_specs = (P("dp", "seq", None), P("dp", None, "seq"), P("dp", "seq"), P(), P(), P("dp", None, "seq"))
    out_specs = (P("dp", "seq"), P("dp", None, "seq"))
    return jax.shard_map(make_device(), mesh=mesh, in_specs=in_specs, out_specs=out_specs, check_vma=False)
```

```python
import jax
import jax.numpy as jnp
from jax import lax
from jax.experimental import pallas as pl
from jax.experimental.pallas import tpu as pltpu
from jax.sharding import PartitionSpec as P

F32, BF16 = jnp.float32, jnp.bfloat16
MESH = pl.DeviceIdType.MESH
D, HD, TXT, SEQ, IMG = 3072, 128, 128, 1152, 1024
HC = 3 * HD
SCALE = HD ** -0.5
LOG2E = 1.4426950408889634
NT = (((1,), (1,)), ((), ()))
TN = (((0,), (0,)), ((), ()))


def dot(a, b, dims=(((1,), (0,)), ((), ()))):
    return lax.dot_general(a, b, dims, preferred_element_type=F32)


def ds(start, size, align):
    return pl.ds(pl.multiple_of(start, align), size)


def project(x, w, joined, first, count, tile):
    def body(t, _):
        r = first + t * tile
        joined[ds(TXT + r, tile, 128), :] = dot(x[ds(r, tile, 128), :], w[...]).astype(BF16)
        return 0

    lax.fori_loop(0, count // tile, body, 0)


def unit_rows(rows):
    rows = rows.astype(F32)
    inverse = lax.rsqrt(jnp.mean(rows * rows, -1, keepdims=True) + 1e-6)
    return rows * inverse, inverse


def attention_start(joined, qg, kg, qn, kn, knt, dk, dv):
    qn[...] = (unit_rows(joined[:, 0:HD])[0] * qg).astype(BF16)
    keys = (unit_rows(joined[:, HD:2 * HD])[0] * kg).astype(BF16)
    kn[...] = keys
    knt[...] = keys.T
    dk[...] = jnp.zeros_like(dk)
    dv[...] = jnp.zeros_like(dv)


def attention_block(joined, dout, qn, kn, knt, dqt, dk, dv, first, count):
    cols = pl.ds(first, count)
    qb, gb = qn[cols, :], dout[cols, :]
    powers = jnp.exp2(dot(kn[...], qb, NT) * (SCALE * LOG2E))
    inverse = 1.0 / jnp.sum(powers, 0, keepdims=True)
    dp = dot(joined[:, 2 * HD:], gb, NT)
    centre = jnp.sum(powers * dp, 0, keepdims=True) * inverse
    probs = (powers * inverse).astype(BF16)
    dscore = (powers * (dp - centre) * (inverse * SCALE)).astype(BF16)
    dv[...] += dot(probs, gb)
    dk[...] += dot(dscore, qb)
    dqt[:, cols] = dot(knt[...], dscore)


def attention_end(joined, qg, kg, dqt, dk, dv, grads):
    for at, gain, grad in ((0, qg, dqt[...].T), (HD, kg, dk[...])):
        unit, inverse = unit_rows(joined[:, at:at + HD])
        grad = grad * gain
        grad = inverse * (grad - unit * jnp.mean(grad * unit, -1, keepdims=True))
        grads[:, at:at + HD] = grad.astype(BF16)
    grads[:, 2 * HD:] = dv[...].astype(BF16)


class Net:
    def __init__(self, send_sems, recv_sems, device):
        self.sems, self.device = (send_sems, recv_sems), device
        self.count, self.groups = 0, {}

    def copy(self, src, dst, send, recv, device):
        return pltpu.make_async_remote_copy(
            src_ref=src, dst_ref=dst, send_sem=self.sems[0].at[send], recv_sem=self.sems[1].at[recv],
            device_id=device, device_id_type=MESH)

    def send(self, src, dst, device, like=None):
        key = len(self.groups) if like is None else id(like)
        index, rows, _ = self.groups.get(key, (len(self.groups), 0, None))
        self.groups[key] = (index, rows + src.shape[0], src if like is None else like)
        copy = self.copy(src, dst, index, self.count, device)
        self.count += 1
        copy.start()
        return copy

    def finish(self):
        for index, rows, ref in self.groups.values():
            ref = ref.at[pl.ds(0, rows)]
            self.copy(ref, ref, index, 0, self.device).wait_send()


PARTS = 4
PROWS = 64 // PARTS
NSEM = 122
NSEND = 16
BQ = 384


def make_kernel():
    def kernel(x_ref, t_ref, w_ref, qg_ref, kg_ref, d_ref, gw_ref, gt_ref,
               xs, wg, joined, grads, dout, qn, kn, knt, dqt, dk, dv, acc, gb,
               from_a, from_b, from_l, from_r, zs, zr, tot, sib_w, sib_t, lsem, done_sem, ssem, rsem):
        dp, seq = lax.axis_index("dp"), lax.axis_index("seq")
        c, zl, y = dp % 2, (dp // 2) % 4, dp // 8
        x, zh = seq % 4, seq // 4
        s = 1 - c
        chip = y * 4 + zl

        def at(yy, zz, cc):
            return {"dp": ((yy % 4) * 4 + zz % 4) * 2 + cc, "seq": seq}

        sib = at(y, zl, s)
        x_right = {"dp": dp, "seq": zh * 4 + (x + 1) % 4}
        x_left = {"dp": dp, "seq": zh * 4 + (x + 3) % 4}
        z_far = {"dp": dp, "seq": (1 - zh) * 4 + x}
        y_right, y_left = at(y + 1, zl, c), at(y + 3, zl, c)
        z_near = [at(y, zl + k, c) for k in (1, 2, 3)]
        qg, kg = qg_ref[...], kg_ref[...]

        local = [
            pltpu.make_async_copy(x_ref, xs.at[c, ds(seq * 128, 128, 128)], lsem.at[0]),
            pltpu.make_async_copy(w_ref.at[:, ds(c * HC, HC, 128)], wg.at[ds(chip * 192 + c * 96, 96, 32)], lsem.at[1]),
            pltpu.make_async_copy(d_ref.at[:, ds(c * HD, HD, 128)], dout.at[c], lsem.at[2]),
            pltpu.make_async_copy(t_ref.at[:, ds(c * HC, HC, 128)], joined.at[c, pl.ds(0, TXT)], lsem.at[3]),
        ]
        for copy in local:
            copy.start()
        barrier = pltpu.get_barrier_semaphore()
        peers = [sib, x_right, x_left, z_far, y_right, y_left] + z_near
        for peer in peers:
            pl.semaphore_signal(barrier, inc=1, device_id=peer, device_id_type=MESH)
        pl.semaphore_wait(barrier, len(peers))
        net = Net(ssem, rsem, sib)
        x_like, w_like, g_like = xs.at[0], wg.at[:], gb.at[:]
        z_like, n_like, s_like, q_like = xs.at[0], wg.at[:], xs.at[0], gb.at[:]

        def xrows(image, slot, half, part=None):
            start = slot * 128 + half * 64
            if part is None:
                return xs.at[image, ds(start, 64, 64)]
            return xs.at[image, ds(start + part * PROWS, PROWS, PROWS)]

        class Ring:
            def __init__(self, image, group):
                self.image = image
                slots = [group * 4 + (x + k) % 4 for k in range(4)]
                self.mine, self.right, self.far, self.left = slots
                self.to_right, self.to_left, self.on = {}, {}, []

            def send(self, part):
                for right in (True, False) if part % 2 == 0 else (False, True):
                    table, device = (self.to_right, x_right) if right else (self.to_left, x_left)
                    block = xrows(self.image, self.mine, c, part)
                    table[part] = net.send(block, block, device, x_like)

            def forward(self, part):
                table, slot, device = (
                    (self.to_right, self.left, x_right) if part % 2 == 0 else (self.to_left, self.right, x_left))
                table[part].wait_recv()
                block = xrows(self.image, slot, c, part)
                self.on.append(net.send(block, block, device, x_like))

            def share_near(self):
                for part in range(PARTS):
                    (self.to_left if part % 2 == 0 else self.to_right)[part].wait_recv()
                self.shared = [share(self.image, slot) for slot in (self.left, self.right)]

            def share_far(self):
                for copy in self.on:
                    copy.wait_recv()
                self.shared.append(share(self.image, self.far))

            def arrived(self):
                for copy in self.shared:
                    copy.wait_recv()

        def share(image, slot):
            block = xrows(image, slot, c)
            return net.send(block, block, sib, s_like)

        w_sib = net.send(w_ref.at[:, ds(s * HC, HC, 128)], wg.at[ds(chip * 192 + c * 96, 96, 32)], sib)
        x_sib = [net.send(x_ref.at[ds(h * 64, 64, 64)], xrows(c, seq, h), sib) for h in (s, c)]
        parts = range(PARTS)
        d_sib = net.send(d_ref.at[:, ds(s * HD, HD, 128)], dout.at[c], sib)
        t_sib = net.send(t_ref.at[:, ds(s * HC, HC, 128)], joined.at[c, pl.ds(0, TXT)], sib)

        y_ring = {}

        def y_send(k):
            block = wg.at[ds((y * 4 + (zl + 4 - k) % 4) * 192, 192, 64)]
            y_ring[k] = [net.send(block, block, device, w_like) for device in (y_right, y_left)]

        def y_forward(k):
            y_ring[k][k % 2].wait_recv()
            step, device = (3, y_right) if k % 2 == 0 else (1, y_left)
            block = wg.at[ds((((y + step) % 4) * 4 + (zl + 4 - k) % 4) * 192, 192, 64)]
            y_ring[k].append(net.send(block, block, device, w_like))

        def y_arrived(k):
            for copy in (y_ring[k][1 - k % 2], y_ring[k][2]):
                copy.wait_recv()

        z = {}

        def z_send(u):
            block = xrows(u // PARTS, seq, c, u % PARTS)
            z[u] = net.send(block, block, z_far, z_like)

        def step(ring, part):
            z[ring.image * PARTS + part].wait_recv()
            ring.send(part)

        local[0].wait()
        x_sib[0].wait_recv()
        own0, own1, ring0, ring1 = Ring(0, zh), Ring(1, zh), Ring(0, 1 - zh), Ring(1, 1 - zh)
        z_send(0)
        for p in parts:
            own0.send(p)
        local[1].wait()
        w_sib.wait_recv()
        block = wg.at[ds(chip * 192, 192, 64)]
        w_near = [net.send(block, block, peer, n_like) for peer in z_near]
        for p in (1, 2, 3):
            z_send(p)
        y_send(0)
        own0.forward(0)
        own0.forward(1)
        step(ring0, 0)
        own0.forward(2)
        own0.forward(3)
        y_forward(0)
        for p in parts:
            own1.send(p)
        own0.share_near()
        step(ring0, 1)
        own0.share_far()
        step(ring0, 2)
        ring0.forward(0)
        w_near[0].wait_recv()
        y_send(1)
        w_near[2].wait_recv()
        y_send(3)
        step(ring0, 3)
        ring0.forward(1)
        w_near[1].wait_recv()
        y_send(2)
        for peer in z_near:
            pl.semaphore_signal(done_sem, inc=1, device_id=peer, device_id_type=MESH)
        pl.semaphore_wait(done_sem, 3)
        for p in parts:
            z_send(PARTS + p)
        far0 = share(0, ring0.mine)
        own1.forward(0)
        ring0.forward(2)
        own1.forward(1)
        y_forward(1)
        ring0.forward(3)
        y_forward(3)
        own1.forward(2)
        y_forward(2)
        ring0.share_near()
        own1.forward(3)
        ring0.share_far()
        step(ring1, 0)
        step(ring1, 1)

        def slots(image, first, count):
            project(xs.at[image], wg, joined.at[image], first * 128, count * 128, count * 128)

        def start(image):
            attention_start(joined.at[image], qg, kg, qn, kn, knt, dk, dv)

        def block(image, i):
            attention_block(joined.at[image], dout.at[image], qn, kn, knt, dqt, dk, dv, i * BQ, BQ)

        def end(image):
            attention_end(joined.at[image], qg, kg, dqt, dk, dv, grads.at[image])

        def early(group):
            cols = ds((group % 4) * 768, 768, 128)
            acc[cols, :] = dot(xs[0, :, cols], grads[0, TXT:, :], TN)

        x_sib[1].wait_recv()
        d_sib.wait_recv()
        t_sib.wait_recv()
        local[2].wait()
        local[3].wait()
        for k in range(4):
            y_arrived(k)
        own0.arrived()
        slots(0, zh * 4, 4)
        own1.share_near()
        step(ring1, 2)
        far0.wait_recv()
        ring0.arrived()
        slots(0, (1 - zh) * 4, 4)
        step(ring1, 3)
        own1.share_far()
        start(0)
        ring1.forward(0)
        block(0, 0)
        ring1.forward(1)
        block(0, 1)
        ring1.forward(2)
        far1 = share(1, ring1.mine)
        block(0, 2)
        ring1.forward(3)
        end(0)
        own1.arrived()
        slots(1, zh * 4, 4)
        ring1.share_near()
        early(y + 2)
        ring1.share_far()
        far1.wait_recv()
        slots(1, ring1.mine, 1)
        for copy, slot in zip(ring1.shared, (ring1.left, ring1.right, ring1.far)):
            copy.wait_recv()
            slots(1, slot, 1)
        start(1)
        for i in range(3):
            block(1, i)
        end(1)
        text = net.send(grads.at[s, pl.ds(0, TXT)], sib_t, sib)

        def late(group):
            cols = ds((group % 4) * 768, 768, 128)
            total = acc[cols, :] + dot(xs[1, :, cols], grads[1, TXT:, :], TN)
            acc[cols, :] = total
            gb[cols, :] = total.astype(BF16)

        right = [(1, 0), (1, 1), (3, 0), (0, 0)]
        left = [(2, 0), (2, 1), (3, 1), (0, 1)]

        def grows(group, piece):
            return ds((group % 4) * 768 + ((zl + piece[0]) % 4) * 192 + piece[1] * 96, 96, 32)

        class Way:
            def __init__(self, ahead, device, far, total, pieces, others):
                self.ahead, self.device, self.far, self.total = ahead, device, far, total
                self.pieces, self.others = pieces, others
                self.far_copy, self.added, self.near = {}, {}, {}

            def send_far(self, i):
                self.far_copy[i] = net.send(gb.at[grows(y + 2, self.pieces[i])], self.far.at[i], self.device, g_like)

            def send_near(self, i):
                self.near[i] = net.send(gb.at[grows(y + self.ahead, self.others[i])], self.total.at[4 + i], self.device, g_like)

            def send_added(self, i):
                self.far_copy[i].wait_recv()
                rows = grows(y + self.ahead, self.pieces[i])
                gb[rows, :] = (acc[rows, :] + self.far[i].astype(F32)).astype(BF16)
                self.added[i] = net.send(gb.at[rows], self.total.at[i], self.device, g_like)

        ways = (Way(1, y_right, from_a, from_l, right, left), Way(3, y_left, from_b, from_r, left, right))
        late(y + 2)
        for i in range(4):
            for way in ways:
                way.send_far(i)
        for step_y in (1, 3, 0):
            early(y + step_y)
            late(y + step_y)
        z_copies = []

        def complete(i):
            for way, other in (ways, ways[::-1]):
                way.added[i].wait_recv()
                other.near[i].wait_recv()
                piece = way.pieces[i]
                rows = grows(y, piece)
                total = acc[rows, :] + way.total[i].astype(F32) + other.total[4 + i].astype(F32)
                k, h = piece
                if k == 0:
                    acc[rows, :] = total
                else:
                    zs[k - 1, pl.ds(h * 96, 96), :] = total.astype(BF16)
                    z_copies.append(net.send(
                        zs.at[k - 1, pl.ds(h * 96, 96)], zr.at[k - 1, pl.ds(h * 96, 96)], z_near[k - 1], q_like))

        for i in range(4):
            for way in ways:
                way.send_added(i)
                way.send_near(i)
            if i >= 1:
                complete(i - 1)
        complete(3)
        for copy in z_copies:
            copy.wait_recv()
        total = acc[ds(chip * 192, 192, 64), :]
        for k in range(3):
            total = total + zr[k].astype(F32)
        tot[...] = total
        last = net.send(tot.at[ds(s * 96, 96, 32)], sib_w, sib)
        gw_ref[:, ds(c * HC, HC, 128)] = tot[ds(c * 96, 96, 32), :]
        last.wait_recv()
        gw_ref[:, ds(s * HC, HC, 128)] = sib_w[...]
        text.wait_recv()
        gt_ref[:, ds(c * HC, HC, 128)] = grads[c, 0:TXT, :]
        gt_ref[:, ds(s * HC, HC, 128)] = sib_t[...]
        net.finish()

    return kernel


def make_device():
    def per_device(x_img, txt_qkv, w_qkv, q_gain, k_gain, d_out):
        hbm, vmem = pl.BlockSpec(memory_space=pl.ANY), pl.BlockSpec(memory_space=pltpu.VMEM)
        grad_w, grad_t = pl.pallas_call(
            make_kernel(),
            name="joint_block",
            out_shape=(jax.ShapeDtypeStruct((96, 2 * HC), F32), jax.ShapeDtypeStruct((TXT, 2 * HC), BF16)),
            in_specs=[hbm, hbm, hbm, vmem, vmem, hbm],
            out_specs=(vmem, vmem),
            scratch_shapes=[
                pltpu.VMEM((2, IMG, D), BF16),
                pltpu.VMEM((D, HC), BF16),
                pltpu.VMEM((2, SEQ, HC), BF16),
                pltpu.VMEM((2, SEQ, HC), BF16),
                pltpu.VMEM((2, SEQ, HD), BF16),
                pltpu.VMEM((SEQ, HD), BF16),
                pltpu.VMEM((SEQ, HD), BF16),
                pltpu.VMEM((HD, SEQ), BF16),
                pltpu.VMEM((HD, SEQ), F32),
                pltpu.VMEM((SEQ, HD), F32),
                pltpu.VMEM((SEQ, HD), F32),
                pltpu.VMEM((D, HC), F32),
                pltpu.VMEM((D, HC), BF16),
                pltpu.VMEM((4, 96, HC), BF16),
                pltpu.VMEM((4, 96, HC), BF16),
                pltpu.VMEM((8, 96, HC), BF16),
                pltpu.VMEM((8, 96, HC), BF16),
                pltpu.VMEM((3, 192, HC), BF16),
                pltpu.VMEM((3, 192, HC), BF16),
                pltpu.VMEM((192, HC), F32),
                pltpu.VMEM((96, HC), F32),
                pltpu.VMEM((TXT, HC), BF16),
                pltpu.SemaphoreType.DMA((4,)),
                pltpu.SemaphoreType.REGULAR,
                pltpu.SemaphoreType.DMA((NSEND,)),
                pltpu.SemaphoreType.DMA((NSEM,)),
            ],
            compiler_params=pltpu.CompilerParams(
                collective_id=0, has_side_effects=True, vmem_limit_bytes=60 * 2 ** 20),
        )(x_img[0], txt_qkv[0], w_qkv, q_gain.reshape(1, HD), k_gain.reshape(1, HD), d_out[0])
        return grad_w, grad_t[None]

    return per_device


def solution(mesh):
    in_specs = (P("dp", "seq", None), P("dp", None, "seq"), P("dp", "seq"), P(), P(), P("dp", None, "seq"))
    out_specs = (P("dp", "seq"), P("dp", None, "seq"))
    return jax.shard_map(make_device(), mesh=mesh, in_specs=in_specs, out_specs=out_specs, check_vma=False)
```

```python
import jax
import jax.numpy as jnp
from jax import lax
from jax.experimental import pallas as pl
from jax.experimental.pallas import tpu as pltpu
from jax.sharding import PartitionSpec as P

F32, BF16 = jnp.float32, jnp.bfloat16
MESH = pl.DeviceIdType.MESH
D, HD, TXT, SEQ, IMG = 3072, 128, 128, 1152, 1024
HC = 3 * HD
SCALE = HD ** -0.5
LOG2E = 1.4426950408889634
NT = (((1,), (1,)), ((), ()))
TN = (((0,), (0,)), ((), ()))


def dot(a, b, dims=(((1,), (0,)), ((), ()))):
    return lax.dot_general(a, b, dims, preferred_element_type=F32)


def ds(start, size, align):
    return pl.ds(pl.multiple_of(start, align), size)


def project(x, w, joined, first, count, tile):
    def body(t, _):
        r = first + t * tile
        joined[ds(TXT + r, tile, 128), :] = dot(x[ds(r, tile, 128), :], w[...]).astype(BF16)
        return 0

    lax.fori_loop(0, count // tile, body, 0)


def unit_rows(rows):
    rows = rows.astype(F32)
    inverse = lax.rsqrt(jnp.mean(rows * rows, -1, keepdims=True) + 1e-6)
    return rows * inverse, inverse


def attention_start(joined, qg, kg, qn, kn, knt):
    qn[...] = (unit_rows(joined[:, 0:HD])[0] * qg).astype(BF16)
    keys = (unit_rows(joined[:, HD:2 * HD])[0] * kg).astype(BF16)
    kn[...] = keys
    knt[...] = keys.T


def attention_block(joined, dout, qn, kn, knt, dqt, dk, dv, first, count):
    cols = pl.ds(first, count)
    qb, gb = qn[cols, :], dout[cols, :]
    powers = jnp.exp2(dot(kn[...], qb, NT) * (SCALE * LOG2E))
    inverse = 1.0 / jnp.sum(powers, 0, keepdims=True)
    dp = dot(joined[:, 2 * HD:], gb, NT)
    centre = jnp.sum(powers * dp, 0, keepdims=True) * inverse
    probs = (powers * inverse).astype(BF16)
    dscore = (powers * (dp - centre) * (inverse * SCALE)).astype(BF16)
    if first == 0:
        dv[...] = dot(probs, gb)
        dk[...] = dot(dscore, qb)
    else:
        dv[...] += dot(probs, gb)
        dk[...] += dot(dscore, qb)
    dqt[:, cols] = dot(knt[...], dscore)


def attention_end(joined, qg, kg, dqt, dk, dv, grads):
    for at, gain, grad in ((0, qg, dqt[...].T), (HD, kg, dk[...])):
        unit, inverse = unit_rows(joined[:, at:at + HD])
        grad = grad * gain
        grad = inverse * (grad - unit * jnp.mean(grad * unit, -1, keepdims=True))
        grads[:, at:at + HD] = grad.astype(BF16)
    grads[:, 2 * HD:] = dv[...].astype(BF16)


class Net:
    def __init__(self, send_sems, recv_sems, device):
        self.sems, self.device = (send_sems, recv_sems), device
        self.count, self.groups = 0, {}

    def copy(self, src, dst, send, recv, device):
        recv = self.sems[1].at[recv] if isinstance(recv, int) else recv
        return pltpu.make_async_remote_copy(
            src_ref=src, dst_ref=dst, send_sem=self.sems[0].at[send], recv_sem=recv,
            device_id=device, device_id_type=MESH)

    def send(self, src, dst, device, like=None, recv=None):
        key = len(self.groups) if like is None else id(like)
        index, rows, _ = self.groups.get(key, (len(self.groups), 0, None))
        self.groups[key] = (index, rows + src.shape[0], src if like is None else like)
        copy = self.copy(src, dst, index, self.count if recv is None else recv, device)
        copy.key = key
        self.count += recv is None
        copy.start()
        return copy

    def sent(self, copy):
        copy.wait_send()
        self.groups[copy.key] = None

    def finish(self):
        for index, rows, ref in filter(None, self.groups.values()):
            ref = ref.at[pl.ds(0, rows)]
            self.copy(ref, ref, index, 0, self.device).wait_send()


PARTS = 4
PROWS = 64 // PARTS
NSEM = 116
NSEND = 16
BQ = 384


def make_kernel():
    def kernel(x_ref, t_ref, w_ref, qg_ref, kg_ref, d_ref, gw_ref, gt_ref,
               xs, wg, joined, grads, dout, qn, kn, knt, dqt, dk, dv, acc, gb,
               from_a, from_b, from_l, from_r, zs, zr, swap, sib_w, sib_t, z_sem, lsem, done_sem, ssem, rsem):
        dp, seq = lax.axis_index("dp"), lax.axis_index("seq")
        c, zl, y = dp % 2, (dp // 2) % 4, dp // 8
        x, zh = seq % 4, seq // 4
        s = 1 - c
        chip = y * 4 + zl

        def at(yy, zz, cc):
            return {"dp": ((yy % 4) * 4 + zz % 4) * 2 + cc, "seq": seq}

        sib = at(y, zl, s)
        x_right = {"dp": dp, "seq": zh * 4 + (x + 1) % 4}
        x_left = {"dp": dp, "seq": zh * 4 + (x + 3) % 4}
        z_far = {"dp": dp, "seq": (1 - zh) * 4 + x}
        y_right, y_left = at(y + 1, zl, c), at(y + 3, zl, c)
        z_near = [at(y, zl + k, c) for k in (1, 2, 3)]
        qg, kg = qg_ref[...], kg_ref[...]

        local = [
            pltpu.make_async_copy(x_ref, xs.at[c, ds(seq * 128, 128, 128)], lsem.at[0]),
            pltpu.make_async_copy(w_ref.at[:, ds(c * HC, HC, 128)], wg.at[ds(chip * 192 + c * 96, 96, 32)], lsem.at[1]),
            pltpu.make_async_copy(d_ref.at[:, ds(c * HD, HD, 128)], dout.at[c], lsem.at[2]),
            pltpu.make_async_copy(t_ref.at[:, ds(c * HC, HC, 128)], joined.at[c, pl.ds(0, TXT)], lsem.at[3]),
        ]
        for copy in local:
            copy.start()
        barrier = pltpu.get_barrier_semaphore()
        z_cross = [at(y, zl + k, s) for k in (1, 2, 3)]
        peers = [sib, x_right, x_left, z_far, y_right, y_left] + z_near + z_cross
        for peer in peers:
            pl.semaphore_signal(barrier, inc=1, device_id=peer, device_id_type=MESH)
        pl.semaphore_wait(barrier, len(peers))
        net = Net(ssem, rsem, sib)
        x_like, w_like, g_like = xs.at[0], wg.at[:], gb.at[:]
        z_like, n_like, s_like, q_like = xs.at[0], wg.at[:], xs.at[0], gb.at[:]

        def xrows(image, slot, half, part=None):
            start = slot * 128 + half * 64
            if part is None:
                return xs.at[image, ds(start, 64, 64)]
            return xs.at[image, ds(start + part * PROWS, PROWS, PROWS)]

        class Ring:
            def __init__(self, image, group):
                self.image = image
                slots = [group * 4 + (x + k) % 4 for k in range(4)]
                self.mine, self.right, self.far, self.left = slots
                self.to_right, self.to_left, self.on = {}, {}, []

            def send(self, part):
                for right in (True, False) if part % 2 == 0 else (False, True):
                    table, device = (self.to_right, x_right) if right else (self.to_left, x_left)
                    block = xrows(self.image, self.mine, c, part)
                    table[part] = net.send(block, block, device, x_like)

            def forward(self, part):
                table, slot, device = (
                    (self.to_right, self.left, x_right) if part % 2 == 0 else (self.to_left, self.right, x_left))
                table[part].wait_recv()
                block = xrows(self.image, slot, c, part)
                self.on.append(net.send(block, block, device, x_like))

            def share_near(self):
                for part in range(PARTS):
                    (self.to_left if part % 2 == 0 else self.to_right)[part].wait_recv()
                self.shared = [share(self.image, slot) for slot in (self.left, self.right)]

            def share_far(self):
                for copy in self.on:
                    copy.wait_recv()
                self.shared.append(share(self.image, self.far))

            def arrived(self):
                for copy in self.shared:
                    copy.wait_recv()

        def share(image, slot):
            block = xrows(image, slot, c)
            return net.send(block, block, sib, s_like)

        w_sib = net.send(w_ref.at[:, ds(s * HC, HC, 128)], wg.at[ds(chip * 192 + c * 96, 96, 32)], sib)
        x_sib = [net.send(x_ref.at[ds(h * 64, 64, 64)], xrows(c, seq, h), sib) for h in (s, c)]
        parts = range(PARTS)
        d_sib = net.send(d_ref.at[:, ds(s * HD, HD, 128)], dout.at[c], sib)
        t_sib = net.send(t_ref.at[:, ds(s * HC, HC, 128)], joined.at[c, pl.ds(0, TXT)], sib)

        y_ring = {}

        def y_send(k):
            block = wg.at[ds((y * 4 + (zl + 4 - k) % 4) * 192, 192, 64)]
            y_ring[k] = [net.send(block, block, device, w_like) for device in (y_right, y_left)]

        def y_forward(k):
            y_ring[k][k % 2].wait_recv()
            step, device = (3, y_right) if k % 2 == 0 else (1, y_left)
            block = wg.at[ds((((y + step) % 4) * 4 + (zl + 4 - k) % 4) * 192, 192, 64)]
            y_ring[k].append(net.send(block, block, device, w_like))

        def y_arrived(k):
            for copy in (y_ring[k][1 - k % 2], y_ring[k][2]):
                copy.wait_recv()

        z = {}

        def z_send(u):
            block = xrows(u // PARTS, seq, c, u % PARTS)
            z[u] = net.send(block, block, z_far, None if u in (4, 5) else z_like)

        def step(ring, part):
            z[ring.image * PARTS + part].wait_recv()
            ring.send(part)

        local[0].wait()
        x_sib[0].wait_recv()
        own0, own1, ring0, ring1 = Ring(0, zh), Ring(1, zh), Ring(0, 1 - zh), Ring(1, 1 - zh)
        z_send(0)
        for p in parts:
            own0.send(p)
        local[1].wait()
        w_sib.wait_recv()
        block = wg.at[ds(chip * 192, 192, 64)]
        w_near = [net.send(block, block, peer, n_like) for peer in z_near]
        for p in (1, 2, 3):
            z_send(p)
        y_send(0)
        own0.forward(0)
        own0.forward(1)
        step(ring0, 0)
        own0.forward(2)
        own0.forward(3)
        y_forward(0)
        for p in parts:
            own1.send(p)
        own0.share_near()
        step(ring0, 1)
        own0.share_far()
        step(ring0, 2)
        ring0.forward(0)
        w_near[0].wait_recv()
        y_send(1)
        w_near[2].wait_recv()
        y_send(3)
        step(ring0, 3)
        ring0.forward(1)
        w_near[1].wait_recv()
        y_send(2)
        for peer in z_near:
            pl.semaphore_signal(done_sem, inc=1, device_id=peer, device_id_type=MESH)
        pl.semaphore_wait(done_sem, 3)
        z_send(4)
        z_send(5)
        far0 = share(0, ring0.mine)
        own1.forward(0)
        ring0.forward(2)
        own1.forward(1)
        y_forward(1)
        ring0.forward(3)
        y_forward(3)
        own1.forward(2)
        y_forward(2)
        ring0.share_near()
        own1.forward(3)
        net.sent(z[4])
        z_send(6)
        net.sent(z[5])
        z_send(7)
        step(ring1, 0)
        step(ring1, 1)
        ring0.share_far()

        def slots(image, first, count):
            project(xs.at[image], wg, joined.at[image], first * 128, count * 128, count * 128)

        def start(image):
            attention_start(joined.at[image], qg, kg, qn, kn, knt)

        def block(image, i):
            attention_block(joined.at[image], dout.at[image], qn, kn, knt, dqt, dk, dv, i * BQ, BQ)

        def end(image):
            attention_end(joined.at[image], qg, kg, dqt, dk, dv, grads.at[image])

        def early(group):
            cols = ds((group % 4) * 768, 768, 128)
            acc[cols, :] = dot(xs[0, :, cols], grads[0, TXT:, :], TN)

        x_sib[1].wait_recv()
        d_sib.wait_recv()
        t_sib.wait_recv()
        local[2].wait()
        local[3].wait()
        for k in range(4):
            y_arrived(k)
        own0.arrived()
        slots(0, zh * 4, 4)
        own1.share_near()
        step(ring1, 2)
        far0.wait_recv()
        ring0.arrived()
        slots(0, (1 - zh) * 4, 4)
        step(ring1, 3)
        own1.share_far()
        start(0)
        ring1.forward(0)
        block(0, 0)
        ring1.forward(1)
        block(0, 1)
        ring1.forward(2)
        far1 = share(1, ring1.mine)
        block(0, 2)
        ring1.forward(3)
        end(0)
        own1.arrived()
        slots(1, zh * 4, 4)
        ring1.share_near()
        early(y + 2)
        ring1.share_far()
        far1.wait_recv()
        slots(1, ring1.mine, 1)
        for copy, slot in zip(ring1.shared, (ring1.left, ring1.right, ring1.far)):
            copy.wait_recv()
            slots(1, slot, 1)
        start(1)
        for i in range(3):
            block(1, i)
        end(1)
        text = net.send(grads.at[s, pl.ds(0, TXT)], sib_t, sib)

        def late(group):
            cols = ds((group % 4) * 768, 768, 128)
            total = acc[cols, :] + dot(xs[1, :, cols], grads[1, TXT:, :], TN)
            acc[cols, :] = total
            gb[cols, :] = total.astype(BF16)

        right = [(1, 0), (1, 1), (3, 0), (0, 0)]
        left = [(2, 0), (2, 1), (3, 1), (0, 1)]

        def grows(group, piece):
            return ds((group % 4) * 768 + ((zl + piece[0]) % 4) * 192 + piece[1] * 96, 96, 32)

        class Way:
            def __init__(self, ahead, device, far, total, pieces, others):
                self.ahead, self.device, self.far, self.total = ahead, device, far, total
                self.pieces, self.others = pieces, others
                self.far_copy, self.added, self.near = {}, {}, {}

            def send_far(self, i):
                self.far_copy[i] = net.send(gb.at[grows(y + 2, self.pieces[i])], self.far.at[i], self.device, g_like)

            def send_near(self, i):
                self.near[i] = net.send(gb.at[grows(y + self.ahead, self.others[i])], self.total.at[4 + i], self.device, g_like)

            def send_added(self, i):
                self.far_copy[i].wait_recv()
                rows = grows(y + self.ahead, self.pieces[i])
                gb[rows, :] = (acc[rows, :] + self.far[i].astype(F32)).astype(BF16)
                self.added[i] = net.send(gb.at[rows], self.total.at[i], self.device, g_like)

        ways = (Way(1, y_right, from_a, from_l, right, left), Way(3, y_left, from_b, from_r, left, right))
        late(y + 2)
        for i in range(4):
            for way in ways:
                way.send_far(i)
        for step_y in (1, 3, 0):
            early(y + step_y)
            late(y + step_y)
        def complete(i):
            for way, other in (ways, ways[::-1]):
                way.added[i].wait_recv()
                other.near[i].wait_recv()
                piece = way.pieces[i]
                rows = grows(y, piece)
                total = acc[rows, :] + way.total[i].astype(F32) + other.total[4 + i].astype(F32)
                k, h = piece
                if k == 0:
                    acc[rows, :] = total
                else:
                    piece = pl.ds(h * 96, 96)
                    zs[k - 1, piece, :] = total.astype(BF16)
                    net.send(zs.at[k - 1, piece], zr.at[c, k - 1], at(y, zl + k, h), q_like, z_sem.at[k - 1, c])

        for i in range(4):
            for way in ways:
                way.send_added(i)
                way.send_near(i)
            if i >= 1:
                complete(i - 1)
        complete(3)
        swap[...] = acc[ds(chip * 192 + s * 96, 96, 32), :].astype(BF16)
        last = net.send(swap, sib_w, sib)
        for k in range(3):
            for core in range(2):
                net.copy(zr.at[core, k], zr.at[core, k], 0, z_sem.at[k, core], sib).wait_recv()
        total = acc[ds(chip * 192 + c * 96, 96, 32), :]
        for k in range(3):
            total = total + zr[c, k].astype(F32)
        gw_ref[:, ds(c * HC, HC, 128)] = total
        last.wait_recv()
        total = sib_w[...].astype(F32)
        for k in range(3):
            total = total + zr[s, k].astype(F32)
        gw_ref[:, ds(s * HC, HC, 128)] = total
        text.wait_recv()
        gt_ref[:, ds(c * HC, HC, 128)] = grads[c, 0:TXT, :]
        gt_ref[:, ds(s * HC, HC, 128)] = sib_t[...]
        net.finish()

    return kernel


def make_device():
    def per_device(x_img, txt_qkv, w_qkv, q_gain, k_gain, d_out):
        hbm, vmem = pl.BlockSpec(memory_space=pl.ANY), pl.BlockSpec(memory_space=pltpu.VMEM)
        grad_w, grad_t = pl.pallas_call(
            make_kernel(),
            name="joint_block",
            out_shape=(jax.ShapeDtypeStruct((96, 2 * HC), F32), jax.ShapeDtypeStruct((TXT, 2 * HC), BF16)),
            in_specs=[hbm, hbm, hbm, vmem, vmem, hbm],
            out_specs=(vmem, vmem),
            scratch_shapes=[
                pltpu.VMEM((2, IMG, D), BF16),
                pltpu.VMEM((D, HC), BF16),
                pltpu.VMEM((2, SEQ, HC), BF16),
                pltpu.VMEM((2, SEQ, HC), BF16),
                pltpu.VMEM((2, SEQ, HD), BF16),
                pltpu.VMEM((SEQ, HD), BF16),
                pltpu.VMEM((SEQ, HD), BF16),
                pltpu.VMEM((HD, SEQ), BF16),
                pltpu.VMEM((HD, SEQ), F32),
                pltpu.VMEM((SEQ, HD), F32),
                pltpu.VMEM((SEQ, HD), F32),
                pltpu.VMEM((D, HC), F32),
                pltpu.VMEM((D, HC), BF16),
                pltpu.VMEM((4, 96, HC), BF16),
                pltpu.VMEM((4, 96, HC), BF16),
                pltpu.VMEM((8, 96, HC), BF16),
                pltpu.VMEM((8, 96, HC), BF16),
                pltpu.VMEM((3, 192, HC), BF16),
                pltpu.VMEM((2, 3, 96, HC), BF16),
                pltpu.VMEM((96, HC), BF16),
                pltpu.VMEM((96, HC), BF16),
                pltpu.VMEM((TXT, HC), BF16),
                pltpu.SemaphoreType.DMA((3, 2)),
                pltpu.SemaphoreType.DMA((4,)),
                pltpu.SemaphoreType.REGULAR,
                pltpu.SemaphoreType.DMA((NSEND,)),
                pltpu.SemaphoreType.DMA((NSEM,)),
            ],
            compiler_params=pltpu.CompilerParams(
                collective_id=0, has_side_effects=True, vmem_limit_bytes=60 * 2 ** 20),
        )(x_img[0], txt_qkv[0], w_qkv, q_gain.reshape(1, HD), k_gain.reshape(1, HD), d_out[0])
        return grad_w, grad_t[None]

    return per_device


def solution(mesh):
    in_specs = (P("dp", "seq", None), P("dp", None, "seq"), P("dp", "seq"), P(), P(), P("dp", None, "seq"))
    out_specs = (P("dp", "seq"), P("dp", None, "seq"))
    return jax.shard_map(make_device(), mesh=mesh, in_specs=in_specs, out_specs=out_specs, check_vma=False)
```

```python
import jax
import jax.numpy as jnp
from jax import lax
from jax.experimental import pallas as pl
from jax.experimental.pallas import tpu as pltpu
from jax.sharding import PartitionSpec as P

F32, BF16 = jnp.float32, jnp.bfloat16
MESH = pl.DeviceIdType.MESH
D, HD, TXT, SEQ, IMG = 3072, 128, 128, 1152, 1024
HC = 3 * HD
SCALE = HD ** -0.5
LOG2E = 1.4426950408889634
NT = (((1,), (1,)), ((), ()))
TN = (((0,), (0,)), ((), ()))


def dot(a, b, dims=(((1,), (0,)), ((), ()))):
    return lax.dot_general(a, b, dims, preferred_element_type=F32)


def ds(start, size, align):
    return pl.ds(pl.multiple_of(start, align), size)


def project(x, w, joined, first, count, tile):
    def body(t, _):
        r = first + t * tile
        joined[ds(TXT + r, tile, 128), :] = dot(x[ds(r, tile, 128), :], w[...]).astype(BF16)
        return 0

    lax.fori_loop(0, count // tile, body, 0)


def unit_rows(rows):
    rows = rows.astype(F32)
    inverse = lax.rsqrt(jnp.mean(rows * rows, -1, keepdims=True) + 1e-6)
    return rows * inverse, inverse


def attention_start(joined, qg, kg, qn, kn, knt):
    qn[...] = (unit_rows(joined[:, 0:HD])[0] * qg).astype(BF16)
    keys = (unit_rows(joined[:, HD:2 * HD])[0] * kg).astype(BF16)
    kn[...] = keys
    knt[...] = keys.T


def attention_block(joined, dout, qn, kn, knt, dqt, dk, dv, first, count):
    cols = pl.ds(first, count)
    qb, gb = qn[cols, :], dout[cols, :]
    powers = jnp.exp2(dot(kn[...], qb, NT) * (SCALE * LOG2E))
    inverse = 1.0 / jnp.sum(powers, 0, keepdims=True)
    dp = dot(joined[:, 2 * HD:], gb, NT)
    centre = jnp.sum(powers * dp, 0, keepdims=True) * inverse
    probs = (powers * inverse).astype(BF16)
    dscore = (powers * (dp - centre) * (inverse * SCALE)).astype(BF16)
    if first == 0:
        dv[...] = dot(probs, gb)
        dk[...] = dot(dscore, qb)
    else:
        dv[...] += dot(probs, gb)
        dk[...] += dot(dscore, qb)
    dqt[:, cols] = dot(knt[...], dscore)


def attention_end(joined, qg, kg, dqt, dk, dv, grads):
    for at, gain, grad in ((0, qg, dqt[...].T), (HD, kg, dk[...])):
        unit, inverse = unit_rows(joined[:, at:at + HD])
        grad = grad * gain
        grad = inverse * (grad - unit * jnp.mean(grad * unit, -1, keepdims=True))
        grads[:, at:at + HD] = grad.astype(BF16)
    grads[:, 2 * HD:] = dv[...].astype(BF16)


class Net:
    def __init__(self, send_sems, recv_sems, device):
        self.sems, self.device = (send_sems, recv_sems), device
        self.count, self.groups = 0, {}

    def copy(self, src, dst, send, recv, device):
        recv = self.sems[1].at[recv] if isinstance(recv, int) else recv
        return pltpu.make_async_remote_copy(
            src_ref=src, dst_ref=dst, send_sem=self.sems[0].at[send], recv_sem=recv,
            device_id=device, device_id_type=MESH)

    def send(self, src, dst, device, like=None, recv=None):
        key = len(self.groups) if like is None else id(like)
        index, rows, _ = self.groups.get(key, (len(self.groups), 0, None))
        self.groups[key] = (index, rows + src.shape[0], src if like is None else like)
        copy = self.copy(src, dst, index, self.count if recv is None else recv, device)
        copy.key = key
        self.count += recv is None
        copy.start()
        return copy

    def sent(self, copy):
        copy.wait_send()
        self.groups[copy.key] = None

    def finish(self):
        for index, rows, ref in filter(None, self.groups.values()):
            ref = ref.at[pl.ds(0, rows)]
            self.copy(ref, ref, index, 0, self.device).wait_send()


PARTS = 4
PROWS = 64 // PARTS
NSEM = 116
NSEND = 16
BQ = 384


def make_kernel():
    def kernel(x_ref, t_ref, w_ref, qg_ref, kg_ref, d_ref, gw_ref, gt_ref,
               xs, wg, joined, grads, dout, qn, kn, knt, dqt, dk, dv, acc, gb,
               from_a, from_b, from_l, from_r, zs, zr, swap, sib_w, sib_t, z_sem, lsem, done_sem, ssem, rsem):
        dp, seq = lax.axis_index("dp"), lax.axis_index("seq")
        c, zl, y = dp % 2, (dp // 2) % 4, dp // 8
        x, zh = seq % 4, seq // 4
        s = 1 - c
        chip = y * 4 + zl

        def at(yy, zz, cc):
            return {"dp": ((yy % 4) * 4 + zz % 4) * 2 + cc, "seq": seq}

        sib = at(y, zl, s)
        x_right = {"dp": dp, "seq": zh * 4 + (x + 1) % 4}
        x_left = {"dp": dp, "seq": zh * 4 + (x + 3) % 4}
        z_far = {"dp": dp, "seq": (1 - zh) * 4 + x}
        y_right, y_left = at(y + 1, zl, c), at(y + 3, zl, c)
        z_near = [at(y, zl + k, c) for k in (1, 2, 3)]
        qg, kg = qg_ref[...], kg_ref[...]

        local = [
            pltpu.make_async_copy(x_ref, xs.at[c, ds(seq * 128, 128, 128)], lsem.at[0]),
            pltpu.make_async_copy(w_ref.at[:, ds(c * HC, HC, 128)], wg.at[ds(chip * 192 + c * 96, 96, 32)], lsem.at[1]),
            pltpu.make_async_copy(d_ref.at[:, ds(c * HD, HD, 128)], dout.at[c], lsem.at[2]),
            pltpu.make_async_copy(t_ref.at[:, ds(c * HC, HC, 128)], joined.at[c, pl.ds(0, TXT)], lsem.at[3]),
        ]
        for copy in local:
            copy.start()
        barrier = pltpu.get_barrier_semaphore()
        z_cross = [at(y, zl + k, s) for k in (1, 2, 3)]
        peers = [sib, x_right, x_left, z_far, y_right, y_left] + z_near + z_cross
        for peer in peers:
            pl.semaphore_signal(barrier, inc=1, device_id=peer, device_id_type=MESH)
        pl.semaphore_wait(barrier, len(peers))
        net = Net(ssem, rsem, sib)
        x_like, w_like, g_like = xs.at[0], wg.at[:], gb.at[:]
        z_like, n_like, s_like, q_like = xs.at[0], wg.at[:], xs.at[0], gb.at[:]

        def xrows(image, slot, half, part=None):
            start = slot * 128 + half * 64
            if part is None:
                return xs.at[image, ds(start, 64, 64)]
            return xs.at[image, ds(start + part * PROWS, PROWS, PROWS)]

        class Ring:
            def __init__(self, image, group, parts):
                self.image, self.parts = image, parts
                slots = [group * 4 + (x + k) % 4 for k in range(4)]
                self.mine, self.right, self.far, self.left = slots
                self.to_right, self.to_left, self.on = {}, {}, []

            def send(self, part, source=None):
                for right in (True, False) if part % 2 == 0 else (False, True):
                    table, device = (self.to_right, x_right) if right else (self.to_left, x_left)
                    block = xrows(self.image, self.mine, c, part)
                    table[part] = net.send(source or block, block, device, x_like)

            def forward(self, part):
                table, slot, device = (
                    (self.to_right, self.left, x_right) if part % 2 == 0 else (self.to_left, self.right, x_left))
                table[part].wait_recv()
                block = xrows(self.image, slot, c, part)
                self.on.append(net.send(block, block, device, x_like))

            def near_wait(self):
                for part in self.parts:
                    (self.to_left if part % 2 == 0 else self.to_right)[part].wait_recv()

            def far_wait(self):
                for copy in self.on:
                    copy.wait_recv()

            def share_near(self):
                self.near_wait()
                self.shared = [share(self.image, slot) for slot in (self.left, self.right)]

            def share_far(self):
                self.far_wait()
                self.shared.append(share(self.image, self.far))

            def arrived(self):
                for copy in self.shared:
                    copy.wait_recv()

        def share(image, slot):
            block = xrows(image, slot, c)
            return net.send(block, block, sib, s_like)

        rest = (1, 2, 3)
        own_c, own_s, part_c, part_s = [Ring(i, g, (0,)) for g in (zh, 1 - zh) for i in (c, s)]
        own0, own1, ring0, ring1 = [Ring(i, g, rest) for g in (zh, 1 - zh) for i in (0, 1)]
        w_sib = net.send(w_ref.at[:, ds(s * HC, HC, 128)], wg.at[ds(chip * 192 + c * 96, 96, 32)], sib)
        x_sib = [net.send(x_ref.at[ds(h * 64, 64, 64)], xrows(c, seq, h), sib) for h in (s, c)]
        block = x_ref.at[ds(c * 64, PROWS, PROWS)]
        own_c.send(0, block)
        z_early = net.send(block, xrows(c, seq, c, 0), z_far, z_like)
        d_sib = net.send(d_ref.at[:, ds(s * HD, HD, 128)], dout.at[c], sib)
        t_sib = net.send(t_ref.at[:, ds(s * HC, HC, 128)], joined.at[c, pl.ds(0, TXT)], sib)

        y_ring = {}

        def y_send(k):
            block = wg.at[ds((y * 4 + (zl + 4 - k) % 4) * 192, 192, 64)]
            y_ring[k] = [net.send(block, block, device, w_like) for device in (y_right, y_left)]

        def y_forward(k):
            y_ring[k][k % 2].wait_recv()
            step, device = (3, y_right) if k % 2 == 0 else (1, y_left)
            block = wg.at[ds((((y + step) % 4) * 4 + (zl + 4 - k) % 4) * 192, 192, 64)]
            y_ring[k].append(net.send(block, block, device, w_like))

        def y_arrived(k):
            for copy in (y_ring[k][1 - k % 2], y_ring[k][2]):
                copy.wait_recv()

        z = {(2, 0): z_early}

        def z_send(image, part, key, source=None):
            block = xrows(image, seq, c, part)
            z[key, part] = net.send(source or block, block, z_far, z_like)

        def step(ring, part, key):
            z[key, part].wait_recv()
            ring.send(part)

        local[0].wait()
        local[1].wait()
        w_sib.wait_recv()
        block = wg.at[ds(chip * 192, 192, 64)]
        w_near = [net.send(block, block, peer, n_like) for peer in z_near]
        x_sib[0].wait_recv()
        own_s.send(0)
        z_send(s, 0, 3)
        for p in rest:
            own0.send(p)
        for p in rest:
            z_send(0, p, 0)
        y_send(0)
        own_c.forward(0)
        own_s.forward(0)
        step(part_c, 0, 2)
        own0.forward(1)
        own0.forward(2)
        own0.forward(3)
        y_forward(0)
        for p in rest:
            own1.send(p)
        own_c.near_wait()
        own_s.near_wait()
        own0.share_near()
        step(part_s, 0, 3)
        own_c.far_wait()
        own_s.far_wait()
        own0.share_far()
        step(ring0, 1, 0)
        part_c.forward(0)
        w_near[0].wait_recv()
        y_send(1)
        w_near[2].wait_recv()
        y_send(3)
        step(ring0, 2, 0)
        part_s.forward(0)
        step(ring0, 3, 0)
        ring0.forward(1)
        w_near[1].wait_recv()
        y_send(2)
        for peer in z_near:
            pl.semaphore_signal(done_sem, inc=1, device_id=peer, device_id_type=MESH)
        pl.semaphore_wait(done_sem, 3)
        for p in rest:
            z_send(1, p, 1)
        far0 = share(0, ring0.mine)
        own1.forward(1)
        ring0.forward(2)
        y_forward(1)
        ring0.forward(3)
        y_forward(3)
        own1.forward(2)
        y_forward(2)
        part_c.near_wait()
        part_s.near_wait()
        ring0.share_near()
        own1.forward(3)
        step(ring1, 1, 1)
        part_c.far_wait()
        part_s.far_wait()
        ring0.share_far()

        def slots(image, first, count):
            project(xs.at[image], wg, joined.at[image], first * 128, count * 128, count * 128)

        def start(image):
            attention_start(joined.at[image], qg, kg, qn, kn, knt)

        def block(image, i):
            attention_block(joined.at[image], dout.at[image], qn, kn, knt, dqt, dk, dv, i * BQ, BQ)

        def end(image):
            attention_end(joined.at[image], qg, kg, dqt, dk, dv, grads.at[image])

        def early(group):
            cols = ds((group % 4) * 768, 768, 128)
            acc[cols, :] = dot(xs[0, :, cols], grads[0, TXT:, :], TN)

        x_sib[1].wait_recv()
        d_sib.wait_recv()
        t_sib.wait_recv()
        local[2].wait()
        local[3].wait()
        for k in range(4):
            y_arrived(k)
        own0.arrived()
        slots(0, zh * 4, 4)
        own1.share_near()
        step(ring1, 2, 1)
        far0.wait_recv()
        ring0.arrived()
        slots(0, (1 - zh) * 4, 4)
        step(ring1, 3, 1)
        own1.share_far()
        start(0)
        block(0, 0)
        ring1.forward(1)
        block(0, 1)
        ring1.forward(2)
        far1 = share(1, ring1.mine)
        block(0, 2)
        ring1.forward(3)
        end(0)
        own1.arrived()
        slots(1, zh * 4, 4)
        ring1.share_near()
        early(y + 2)
        ring1.share_far()
        far1.wait_recv()
        slots(1, ring1.mine, 1)
        for copy, slot in zip(ring1.shared, (ring1.left, ring1.right, ring1.far)):
            copy.wait_recv()
            slots(1, slot, 1)
        start(1)
        for i in range(3):
            block(1, i)
        end(1)
        text = net.send(grads.at[s, pl.ds(0, TXT)], sib_t, sib)

        def late(group):
            cols = ds((group % 4) * 768, 768, 128)
            total = acc[cols, :] + dot(xs[1, :, cols], grads[1, TXT:, :], TN)
            acc[cols, :] = total
            gb[cols, :] = total.astype(BF16)

        right = [(1, 0), (1, 1), (3, 0), (0, 0)]
        left = [(2, 0), (2, 1), (3, 1), (0, 1)]

        def grows(group, piece):
            return ds((group % 4) * 768 + ((zl + piece[0]) % 4) * 192 + piece[1] * 96, 96, 32)

        class Way:
            def __init__(self, ahead, device, far, total, pieces, others):
                self.ahead, self.device, self.far, self.total = ahead, device, far, total
                self.pieces, self.others = pieces, others
                self.far_copy, self.added, self.near = {}, {}, {}

            def send_far(self, i):
                self.far_copy[i] = net.send(gb.at[grows(y + 2, self.pieces[i])], self.far.at[i], self.device, g_like)

            def send_near(self, i):
                self.near[i] = net.send(gb.at[grows(y + self.ahead, self.others[i])], self.total.at[4 + i], self.device, g_like)

            def send_added(self, i):
                self.far_copy[i].wait_recv()
                rows = grows(y + self.ahead, self.pieces[i])
                gb[rows, :] = (acc[rows, :] + self.far[i].astype(F32)).astype(BF16)
                self.added[i] = net.send(gb.at[rows], self.total.at[i], self.device, g_like)

        ways = (Way(1, y_right, from_a, from_l, right, left), Way(3, y_left, from_b, from_r, left, right))
        late(y + 2)
        for i in range(4):
            for way in ways:
                way.send_far(i)
        for step_y in (1, 3, 0):
            early(y + step_y)
            late(y + step_y)
        def complete(i):
            for way, other in (ways, ways[::-1]):
                way.added[i].wait_recv()
                other.near[i].wait_recv()
                piece = way.pieces[i]
                rows = grows(y, piece)
                total = acc[rows, :] + way.total[i].astype(F32) + other.total[4 + i].astype(F32)
                k, h = piece
                if k == 0:
                    acc[rows, :] = total
                else:
                    piece = pl.ds(h * 96, 96)
                    zs[k - 1, piece, :] = total.astype(BF16)
                    net.send(zs.at[k - 1, piece], zr.at[c, k - 1], at(y, zl + k, h), q_like, z_sem.at[k - 1, c])

        for i in range(4):
            for way in ways:
                way.send_added(i)
                way.send_near(i)
            if i >= 1:
                complete(i - 1)
        complete(3)
        swap[...] = acc[ds(chip * 192 + s * 96, 96, 32), :].astype(BF16)
        last = net.send(swap, sib_w, sib)
        for k in range(3):
            for core in range(2):
                net.copy(zr.at[core, k], zr.at[core, k], 0, z_sem.at[k, core], sib).wait_recv()
        total = acc[ds(chip * 192 + c * 96, 96, 32), :]
        for k in range(3):
            total = total + zr[c, k].astype(F32)
        gw_ref[:, ds(c * HC, HC, 128)] = total
        last.wait_recv()
        total = sib_w[...].astype(F32)
        for k in range(3):
            total = total + zr[s, k].astype(F32)
        gw_ref[:, ds(s * HC, HC, 128)] = total
        text.wait_recv()
        gt_ref[:, ds(c * HC, HC, 128)] = grads[c, 0:TXT, :]
        gt_ref[:, ds(s * HC, HC, 128)] = sib_t[...]
        net.finish()

    return kernel


def make_device():
    def per_device(x_img, txt_qkv, w_qkv, q_gain, k_gain, d_out):
        hbm, vmem = pl.BlockSpec(memory_space=pl.ANY), pl.BlockSpec(memory_space=pltpu.VMEM)
        grad_w, grad_t = pl.pallas_call(
            make_kernel(),
            name="joint_block",
            out_shape=(jax.ShapeDtypeStruct((96, 2 * HC), F32), jax.ShapeDtypeStruct((TXT, 2 * HC), BF16)),
            in_specs=[hbm, hbm, hbm, vmem, vmem, hbm],
            out_specs=(vmem, vmem),
            scratch_shapes=[
                pltpu.VMEM((2, IMG, D), BF16),
                pltpu.VMEM((D, HC), BF16),
                pltpu.VMEM((2, SEQ, HC), BF16),
                pltpu.VMEM((2, SEQ, HC), BF16),
                pltpu.VMEM((2, SEQ, HD), BF16),
                pltpu.VMEM((SEQ, HD), BF16),
                pltpu.VMEM((SEQ, HD), BF16),
                pltpu.VMEM((HD, SEQ), BF16),
                pltpu.VMEM((HD, SEQ), F32),
                pltpu.VMEM((SEQ, HD), F32),
                pltpu.VMEM((SEQ, HD), F32),
                pltpu.VMEM((D, HC), F32),
                pltpu.VMEM((D, HC), BF16),
                pltpu.VMEM((4, 96, HC), BF16),
                pltpu.VMEM((4, 96, HC), BF16),
                pltpu.VMEM((8, 96, HC), BF16),
                pltpu.VMEM((8, 96, HC), BF16),
                pltpu.VMEM((3, 192, HC), BF16),
                pltpu.VMEM((2, 3, 96, HC), BF16),
                pltpu.VMEM((96, HC), BF16),
                pltpu.VMEM((96, HC), BF16),
                pltpu.VMEM((TXT, HC), BF16),
                pltpu.SemaphoreType.DMA((3, 2)),
                pltpu.SemaphoreType.DMA((4,)),
                pltpu.SemaphoreType.REGULAR,
                pltpu.SemaphoreType.DMA((NSEND,)),
                pltpu.SemaphoreType.DMA((NSEM,)),
            ],
            compiler_params=pltpu.CompilerParams(
                collective_id=0, has_side_effects=True, vmem_limit_bytes=60 * 2 ** 20),
        )(x_img[0], txt_qkv[0], w_qkv, q_gain.reshape(1, HD), k_gain.reshape(1, HD), d_out[0])
        return grad_w, grad_t[None]

    return per_device


def solution(mesh):
    in_specs = (P("dp", "seq", None), P("dp", None, "seq"), P("dp", "seq"), P(), P(), P("dp", None, "seq"))
    out_specs = (P("dp", "seq"), P("dp", None, "seq"))
    return jax.shard_map(make_device(), mesh=mesh, in_specs=in_specs, out_specs=out_specs, check_vma=False)
```
